128 devices in a mesh: dp: 4 (over x), expert: 8 (over z, core), mp: 4 (over y).
Axes of the slice: x: 4, y: 4, z: 4, core: 2. Of those that a mesh axis runs over, the one named last changes fastest.
Arguments:
- tokens: bfloat16 [8192, 2048], P(('dp', 'expert')), may hold values from -6 to 6
- attn_norm: float32 [2048], replicated, may hold values from 0.5 to 1.5
- qkv_weights: bfloat16 [3, 2048, 2048], P(None, ('dp', 'expert'), 'mp'), may hold values from -0.125 to 0.125
- out_weight: bfloat16 [2048, 2048], P(('dp', 'expert'), 'mp'), may hold values from -0.5 to 0.5
- q_gain: float32 [2048], P('mp'), may hold values from 0.1 to 1.9
- k_gain: float32 [2048], P('mp'), may hold values from 0.1 to 1.9
- ffn_norm: float32 [2048], replicated, may hold values from 0.5 to 1.5
- router: bfloat16 [2048, 64], replicated, may hold values from -0.0625 to 0.0625
- expert_weights: bfloat16 [64, 3, 2048, 1024], P(('dp', 'expert'), None, None, 'mp'), may hold values from -6 to 6
- lengths: int32 [32, 4], P(('dp', 'expert')), may hold values from 1 to 192, 256 in all within a row
- expert_ids: int32 [8192, 8], P(('dp', 'expert')), may hold values from 0 to 63, all different within a row; in each aligned block of 256 rows (0 to 255, 256 to 511, ...) at most 48 rows name the same one
- cotangent: bfloat16 [8192, 2048], P(('dp', 'expert')), may hold values from -6 to 6
Outputs:
- out: bfloat16 [8192, 2048], P(('dp', 'expert'))
- input_grad: float32 [8192, 2048], P(('dp', 'expert'))
- grad_attn_norm: float32 [2048], replicated
- grad_qkv: float32 [3, 2048, 2048], P(None, ('dp', 'expert'), 'mp')
- grad_out_weight: float32 [2048, 2048], P(('dp', 'expert'), 'mp')
- grad_q_gain: float32 [2048], P('mp')
- grad_k_gain: float32 [2048], P('mp')
- grad_ffn_norm: float32 [2048], replicated
- grad_router: float32 [2048, 64], replicated
- grad_experts: float32 [64, 2, 2048, 1024], P(('dp', 'expert'), None, None, 'mp')
- grad_down: float32 [64, 2048, 1024], P(('dp', 'expert'), None, 'mp')
The draws below stay inside these ranges and needn't reach their ends.
Inputs may be any that keep to these rules, and one draw needn't show every extreme that they name: `expert_ids`: each row names 8 different experts. Within each aligned block of 256 rows (one token group) no expert is named by more than 48 rows, and in some block an expert is named by exactly 48. `lengths`: each row sums to 256, and its largest entry is 192.
All inputs are finite; a program needn't handle non-finite values.
Results may differ from the reference program's by a relative error of at most 0.025.
Values may be sent and summed in bfloat16 or wider, within the bound.
A program may use at most 256 MiB of HBM per device.

```python
import math
import jax
import jax.numpy as jnp
import numpy as np
from jax import lax

D = 2048
HEADS = 16
HEAD = 128
FF = 1024
EXPERTS = 64
TOP = 8
TOK_GRP = 256
SEQS = 4
SEQ_MOST = 192
HD = 2048
GROUPS = 32
TOKENS = 8192
CAP = 48
N_DP = 4
N_EXPERT = 8


def draw_expert_weights(key, part):
    key = jax.random.fold_in(key, 17)
    shape = (EXPERTS, 3, D, FF)
    base = jnp.clip(jax.random.normal(key, shape, jnp.float32), -5.0, 5.0)
    factor = jnp.where(jnp.arange(3) == 2, 1.2, D ** (-0.5)).astype(jnp.float32)
    return (base * factor[None, :, None, None]).astype(jnp.bfloat16)


def level_of(own_key, dims, shards, least, high):
    def one(dim, shards_of):
        draws = jax.random.uniform(jax.random.fold_in(jax.random.fold_in(own_key, 6), dim), (shards_of,), jnp.float32, least / len(shards), high / len(shards))
        return jnp.repeat(jnp.exp(draws), dims[dim] // shards_of).reshape((-1,) + (1,) * (len(dims) - dim - 1))

    loudness = one(*shards[0])
    for cut in shards[1:]:
        loudness = loudness * one(*cut)
    return loudness


def split_up(number_of, total, limit, slope):
    loads = [(1 << 20) // math.isqrt(rank ** slope) + 1 for rank in range(2, number_of + 1)]
    surplus, given = total - limit - (number_of - 1), [1] * (number_of - 1)
    while surplus > 0:
        movable = [i for i in range(number_of - 1) if given[i] < limit]
        whole, budget = sum([loads[i] for i in movable]), surplus
        for i in movable:
            extra = min(limit - given[i], max(1, budget * loads[i] // whole), surplus)
            given[i] = given[i] + extra
            surplus = surplus - extra
    return np.array([limit] + given)


def ragged_sizes(key, amount, total, reach, slope):
    if amount == 2:
        one = jax.random.randint(key, (), max(1, total - reach), min(reach, total - 1) + 1)
        return jnp.stack([one, total - one])
    tallies = jnp.asarray(split_up(amount, total, reach, slope), jnp.int32)
    couples = (amount - 1) // 2
    source_of, receiver = tallies[1:1 + 2 * couples:2], tallies[2:2 + 2 * couples:2]
    slack = jnp.minimum(source_of - 1, reach - receiver)
    passed = jax.random.randint(jax.random.fold_in(key, 1), (couples,), 0, 1 << 20) % (slack + 1)
    tallies = tallies.at[1:1 + 2 * couples:2].set(source_of - passed).at[2:2 + 2 * couples:2].set(receiver + passed)
    return tallies[jax.random.permutation(jax.random.fold_in(key, 2), amount)]


def deal_out(stream_key, own, number, rows, amount, top, limit, skew):
    order = jax.random.permutation(stream_key, amount)
    crowded, ordinary = shares(amount, rows * top, limit, skew, True), shares(amount, rows * top, limit, skew, False)
    places = jnp.arange(amount)

    def named(tallies, rotation):
        used = int((tallies > 0).sum())
        fixed = max(1, used // 4)
        shifted = fixed + (places - fixed + rotation * (used - fixed)) % max(1, amount - fixed)
        return jnp.zeros((amount,), jnp.int32).at[order[jnp.where(places < fixed, places, shifted)]].set(jnp.asarray(tallies, jnp.int32))

    tallies = jnp.where(number % 4 == 0, named(crowded, number // 4), named(ordinary, number - number // 4 - 1))
    mixed = jax.random.permutation(jax.random.fold_in(own, 3), amount)
    giver, taker = mixed[0:amount // 2 * 2:2], mixed[1:amount // 2 * 2:2]
    room = jnp.minimum(tallies[giver] - 1, limit - tallies[taker]) // 2
    room = jnp.where((giver == order[0]) | (taker == order[0]) | (tallies[taker] == 0), 0, jnp.maximum(room, 0))
    shifted = jax.random.randint(jax.random.fold_in(own, 4), (amount // 2,), 0, 1 << 20) % (room + 1)
    tallies = tallies.at[giver].add(-shifted).at[taker].add(shifted)
    items = jnp.searchsorted(jnp.cumsum(tallies), jnp.arange(rows * top), side="right").astype(jnp.int32)
    table = items.reshape(top, rows).T
    table = table[jax.random.permutation(jax.random.fold_in(own, 1), rows)]
    rotation = jax.random.randint(jax.random.fold_in(own, 2), (rows, 1), 0, top)
    return jnp.take_along_axis(table, (jnp.arange(top)[None, :] + rotation) % top, axis=1)


def shares(count, total, most, skew, full):
    portions = [(1 << 20) // math.isqrt(grade ** skew) + 1 for grade in range(1, count + 1)]
    largest = most if full else min(most, max(-(-total // count), total * portions[0] // sum(portions)))
    least = 1 if total - largest >= count - 1 else 0
    given, rest = [largest] + [least] * (count - 1), total - largest - least * (count - 1)
    while rest > 0:
        candidates = [i for i in range(1, count) if given[i] < largest] or [i for i in range(1, count) if given[i] < most]
        mass, budget = sum([portions[i] for i in candidates]), rest
        for i in candidates:
            extra = min(most - given[i], max(1, budget * portions[i] // mass), rest)
            given[i] = given[i] + extra
            rest = rest - extra
    return np.array(given)


def bell_draw(key, extent, deviation, bound, pieces=(), kind=jnp.bfloat16):
    drawn = jax.random.normal(key, extent, jnp.float32) * deviation
    if len(pieces) > 0:
        drawn = level_of(key, extent, pieces, -0.22, 0.18) * drawn
    return jnp.clip(drawn, min=-bound, max=bound).astype(kind)


def setup_inputs(seed: int = 0) -> dict:
    splits = jax.random.split(jax.random.key(seed), 13)
    tokens = bell_draw(splits[0], (TOKENS, D), 1.0, 6.0, ((0, 32),))
    attn_norm = jnp.clip(1.0 + 0.1 * jax.random.normal(splits[1], (D,), jnp.float32), 0.5, 1.5)
    qkv_weights = bell_draw(splits[2], (3, D, HD), D ** -0.5, 0.125, ((1, 32), (2, 4)))
    out_weight = bell_draw(splits[3], (D, HD), (HD // 16) ** -0.5, 0.5, ((0, 32), (1, 4)))
    q_gain = jnp.clip(1.0 + 0.18 * jax.random.normal(splits[4], (HD,), jnp.float32), 0.1, 1.9)
    k_gain = jnp.clip(1.0 + 0.18 * jax.random.normal(splits[5], (HD,), jnp.float32), 0.1, 1.9)
    ffn_norm = jnp.clip(1.0 + 0.1 * jax.random.normal(splits[6], (D,), jnp.float32), 0.5, 1.5)
    router = bell_draw(splits[7], (D, EXPERTS), (4 * D) ** -0.5, 0.0625)
    expert_weights = draw_expert_weights(jax.random.fold_in(splits[12], 71), 0)
    lengths = jax.vmap(lambda own: ragged_sizes(own, SEQS, TOK_GRP, SEQ_MOST, 2))(jax.random.split(splits[9], GROUPS)).reshape((GROUPS, SEQS)).astype(jnp.int32)
    expert_ids_keys = jax.random.split(jax.random.fold_in(splits[10], 1), TOKENS // TOK_GRP)
    expert_ids_turns = jax.random.permutation(jax.random.fold_in(splits[10], 3), TOKENS // TOK_GRP)
    expert_ids = jax.vmap(lambda own, number: deal_out(jax.random.fold_in(splits[10], 2), own, number, TOK_GRP, EXPERTS, TOP, CAP, 1))(expert_ids_keys, expert_ids_turns).reshape((TOKENS, TOP))
    cotangent = bell_draw(splits[11], (TOKENS, D), 1.0, 6.0, ((0, 32),))
    return dict(tokens=tokens, attn_norm=attn_norm, qkv_weights=qkv_weights, out_weight=out_weight, q_gain=q_gain, k_gain=k_gain, ffn_norm=ffn_norm, router=router, expert_weights=expert_weights, lengths=lengths, expert_ids=expert_ids, cotangent=cotangent)


@jax.custom_vjp
def low(v):
    return lax.optimization_barrier(v.astype(jnp.bfloat16)).astype(jnp.float32)

@jax.custom_vjp
def low_back(v):
    return v

def low_keep(v):
    return (low(v), None)

def low_pass(kept, grad):
    return (grad,)

def back_keep(v):
    return (v, None)

def back_low(kept, grad):
    return (low(grad),)
low.defvjp(low_keep, low_pass)
low_back.defvjp(back_keep, back_low)
EPSILON = 1e-05
HIGHEST = lax.Precision.HIGHEST

def rms_gain(values, gain):
    return values * lax.rsqrt(lax.optimization_barrier(jnp.mean(values * values, axis=-1, keepdims=True)) + EPSILON) * gain

def rope_tables(position):
    half = HEAD // 2
    freqs = 10000.0 ** (-jnp.arange(half, dtype=jnp.float32) / half)
    angles = position.astype(jnp.float32)[:, None] * freqs[None, :]
    return (jnp.cos(angles)[:, None, :], jnp.sin(angles)[:, None, :])

def rotate(values, cosine, sine):
    half = HEAD // 2
    first = values[..., :half]
    second = values[..., half:]
    return jnp.concatenate([first * cosine - second * sine, second * cosine + first * sine], axis=-1)

def layout(lengths_row):
    index = jnp.arange(TOK_GRP, dtype=jnp.int32)
    ends = jnp.cumsum(lengths_row, dtype=jnp.int32)
    starts = ends - lengths_row
    segment = lax.optimization_barrier(jnp.sum((index[:, None] >= ends[None, :]).astype(jnp.int32), axis=1, dtype=jnp.int32))
    chosen = segment[:, None] == jnp.arange(SEQS, dtype=jnp.int32)[None, :]
    position = index - lax.optimization_barrier(jnp.sum(jnp.where(chosen, starts[None, :], 0), axis=1, dtype=jnp.int32))
    allowed = (segment[:, None] == segment[None, :]) & (index[None, :] <= index[:, None])
    return (position, allowed)

def slots_of(ids_group):
    flat = ids_group.reshape(-1)
    onehot = (flat[:, None] == jnp.arange(EXPERTS, dtype=jnp.int32)[None, :]).astype(jnp.int32)
    before = jnp.cumsum(onehot, axis=0, dtype=jnp.int32) - onehot
    return (flat, lax.optimization_barrier(jnp.sum(before * onehot, axis=1, dtype=jnp.int32)))

def group_forward(params, inputs):
    attn_norm, qkv_weights, out_weight, q_gain, k_gain, ffn_norm, router, expert_weights = params
    hidden_in, lengths_row, ids_group = inputs
    position, allowed = layout(lengths_row)
    cosine, sine = rope_tables(position)
    normed = low(rms_gain(hidden_in, attn_norm))
    query = low_back(jnp.dot(normed, qkv_weights[0], precision=HIGHEST))
    key_proj = low_back(jnp.dot(normed, qkv_weights[1], precision=HIGHEST))
    value = low_back(jnp.dot(normed, qkv_weights[2], precision=HIGHEST))
    query_heads = rms_gain(query, q_gain).reshape(TOK_GRP, HEADS, HEAD)
    key_heads = rms_gain(key_proj, k_gain).reshape(TOK_GRP, HEADS, HEAD)
    query_rot = low(rotate(query_heads, cosine, sine))
    key_rot = low(rotate(key_heads, cosine, sine))
    value_heads = low(value).reshape(TOK_GRP, HEADS, HEAD)
    scores = low_back(jnp.einsum('qhc,khc->hqk', query_rot, key_rot, precision=HIGHEST) * HEAD ** (-0.5))
    scores = jnp.where(allowed[None], scores, -1e+30)
    probs = low(jax.nn.softmax(scores, axis=-1))
    mixed = low(low_back(jnp.einsum('hqk,khc->qhc', probs, value_heads, precision=HIGHEST)))
    mixed = mixed.reshape(TOK_GRP, HD)
    attn_out = low_back(jnp.einsum('tc,dc->td', mixed, out_weight, precision=HIGHEST))
    resid = hidden_in + attn_out
    moe_in = low(rms_gain(resid, ffn_norm))
    logits = low_back(jnp.dot(moe_in, router, precision=HIGHEST))
    weights = jax.nn.softmax(logits, axis=-1)
    gates = jnp.take_along_axis(weights, ids_group, axis=1)
    flat, slot = slots_of(ids_group)
    dest = flat * CAP + slot
    buffer = jnp.zeros((EXPERTS * CAP, D), jnp.float32).at[dest].set(jnp.repeat(moe_in, TOP, axis=0))
    buffer = buffer.reshape(EXPERTS, CAP, D)
    gate_pre = low_back(jnp.einsum('ecd,edf->ecf', buffer, expert_weights[:, 0], precision=HIGHEST))
    up_pre = low_back(jnp.einsum('ecd,edf->ecf', buffer, expert_weights[:, 1], precision=HIGHEST))
    inner = low(jax.nn.silu(gate_pre) * up_pre)
    expert_out = low(low_back(jnp.einsum('ecf,edf->ecd', inner, expert_weights[:, 2], precision=HIGHEST)))
    picked = expert_out.reshape(EXPERTS * CAP, D)[dest].reshape(TOK_GRP, TOP, D)
    return resid + lax.optimization_barrier(jnp.sum(gates[:, :, None] * picked, axis=1))

def reference(tokens, attn_norm, qkv_weights, out_weight, q_gain, k_gain, ffn_norm, router, expert_weights, lengths, expert_ids, cotangent):
    params = tuple((piece.astype(jnp.float32) for piece in (attn_norm, qkv_weights, out_weight, q_gain, k_gain, ffn_norm, router, expert_weights)))
    hidden = tokens.astype(jnp.float32)
    groups = N_DP * N_EXPERT

    def forward(params, hidden):

        def advance(carry, inputs):
            return (carry, jax.checkpoint(group_forward)(params, inputs))
        stacked = (hidden.reshape(groups, TOK_GRP, D), lengths, expert_ids.reshape(groups, TOK_GRP, TOP))
        _, outputs = lax.scan(advance, jnp.zeros((), jnp.float32), stacked)
        return outputs.reshape(groups * TOK_GRP, D)
    output, pullback = jax.vjp(forward, params, hidden)
    grads, input_grad = pullback(cotangent.astype(jnp.float32))
    return (output.astype(jnp.bfloat16), input_grad, grads[0], grads[1], grads[2], grads[3], grads[4], grads[5], grads[6], grads[7][:, :2], grads[7][:, 2])
```

```python
import functools

import jax
import jax.numpy as jnp
from jax import lax
from jax.experimental import pallas as pl
from jax.experimental.pallas import tpu as pltpu
from jax.sharding import PartitionSpec as P

HEADS = 16
HEAD = 128
TOK = 256
SEQS = 4
EXPERTS = 64
CAP = 48
VMEM_LIMIT = 60 * 1024 * 1024


EPSILON = 1e-05


def dot(a, b, dims):
    return lax.dot_general(a, b, (dims, ((), ())), preferred_element_type=jnp.float32)


NN = ((1,), (0,))
NT = ((1,), (1,))
TN = ((0,), (0,))


RING = 4
X, Z, Y = 0, 1, 2


def place():
    x, e, y = (lax.axis_index(name) for name in ("dp", "expert", "mp"))
    return (x, e // 2, y), e % 2


def device_at(axis, at, core):
    return {X: {"dp": at}, Z: {"expert": at * 2 + core}, Y: {"mp": at}}[axis]


class Links:
    def __init__(self, axes, send_sems, recv_sems, pair=False, extra=()):
        self.at, self.core = place()
        self.send_sems, self.recv_sems, self.used, self.open = send_sems, recv_sems, 0, {}
        self.ended = set()
        barrier = pltpu.get_barrier_semaphore()
        peers = [self.peer(axis, step) for axis in axes for step in (1, -1)]
        peers += [self.peer(axis, step) for axis, step in extra]
        if pair:
            peers.append(self.pair())
        for peer in peers:
            pl.semaphore_signal(
                barrier, inc=1, device_id=peer, device_id_type=pl.DeviceIdType.MESH
            )
        pl.semaphore_wait(barrier, len(peers))

    def rel(self, axis, step):
        return lax.rem(self.at[axis] + (step + RING), RING)

    def peer(self, axis, step):
        return device_at(axis, self.rel(axis, step), self.core)

    def pair(self):
        return {"expert": self.at[Z] * 2 + (1 - self.core)}

    def copy(self, k, src, dst, peer):
        return pltpu.make_async_remote_copy(
            src_ref=src,
            dst_ref=dst,
            send_sem=self.send_sems.at[k],
            recv_sem=self.recv_sems.at[k],
            device_id=peer,
            device_id_type=pl.DeviceIdType.MESH,
        )

    def reserve(self):
        k = self.used
        assert k < self.send_sems.shape[0]
        self.used += 1
        return k

    def send(self, src, dst, peer, k=None):
        k = self.reserve() if k is None else k
        dst = dst() if callable(dst) else dst
        self.copy(k, src() if callable(src) else src, dst, peer).start()
        self.open[k] = src
        return k

    def sent(self, k, src):
        src = src() if callable(src) else src
        self.copy(k, src, src, self.pair()).wait_send()
        self.ended.add(k)

    def arrive(self, k, dst):
        self.copy(k, dst, dst, self.pair()).wait_recv()

    def close(self):
        for k, src in self.open.items():
            if k not in self.ended:
                self.sent(k, src)


def run_all(steps):
    steps = list(steps)
    while steps:
        steps = [s for s in steps if next(s, "end") != "end"]


def gather_part(links, view, shard, order, forward=None, late=False):
    mine = [links.at[axis] for axis in order]
    n = len(order)
    arrived = [{} for _ in order]
    held = []

    def region(i, c, step, half=None):
        places = {}
        for j, axis in enumerate(order):
            if j == i:
                places[axis] = links.rel(axis, step)
            elif j > i:
                places[axis] = mine[j]
            elif j == i - 1 and c is not None:
                places[axis] = links.rel(axis, c)
        return view(places, half)

    def own(i, c):
        if late and i == n - 1 and c not in held:
            held.append(c)
            return
        src = shard if i == 0 or (i == 1 and c == 0) else region(i, c, 0)
        for step in (1, -1):
            k = links.send(src, region(i, c, 0), links.peer(order[i], step))
            arrived[i][c, -step] = k

    def onward(i, c, step):
        links.arrive(arrived[i][c, step], region(i, c, step))
        half = 0 if step == -1 else 1
        part = region(i, c, step, half)
        arrived[i][c, 2, half] = links.send(part, part, links.peer(order[i], -step))

    def opposite(i, c):
        for half in (0, 1):
            links.arrive(arrived[i][c, 2, half], region(i, c, 2, half))

    for i in range(n):
        chunks = [None] if i == 0 else [0, -1, 1, 2]
        if late and i == n - 1:
            for c in chunks:
                own(i, c)
            yield
        if i == 0:
            own(0, None)
            if forward:
                forward(shard, region(0, None, 0))
            if n > 1:
                own(1, 0)
            yield
        for step in (-1, 1):
            for c in chunks:
                onward(i, c, step)
            if i + 1 < n:
                own(i + 1, step)
            if forward:
                forward(region(i, None, step), region(i, None, step))
            yield
        for c in chunks:
            opposite(i, c)
        if i + 1 < n:
            own(i + 1, 2)
        if i + 2 < n:
            own(i + 2, 0)
        if forward:
            forward(region(i, None, 2), region(i, None, 2))
        yield


def cut_as(*tiles):
    return [(sum(tiles[:i]) * 128, size * 128) for i, size in enumerate(tiles)]


def add_into(dst, *others):
    def one(d, *refs):
        total = d[...].astype(jnp.float32)
        for ref in refs:
            total = total + ref[...].astype(jnp.float32)
        d[...] = total.astype(d.dtype)

    if len(dst.shape) == 2:
        one(dst, *others)
    else:

        @pl.loop(0, dst.shape[0])
        def _(i):
            one(dst.at[i], *(ref.at[i] for ref in others))


def halves(ref, half):
    rows = ref.shape[-2]
    cut = pl.ds(half * (rows // 2), rows // 2)
    return ref.at[cut] if len(ref.shape) == 2 else ref.at[:, cut]


def reduce_axis(links, axis, opp, right, left, own, passing, landing, ready=None):
    to_right, to_left = links.peer(axis, 1), links.peer(axis, -1)
    k_a = links.send(halves(opp, 0), passing.at[0], to_right)
    k_b = links.send(halves(opp, 1), passing.at[1], to_left)
    k_c = links.send(halves(right[0], 1), halves(landing.at[0], 1), to_right)
    k_d = links.send(halves(left[0], 0), halves(landing.at[1], 0), to_left)
    yield
    if ready is not None:
        ready()
    links.arrive(k_a, passing.at[0])
    add_into(passing.at[0], right[1])
    k_e = links.send(passing.at[0], halves(landing.at[0], 0), to_right)
    links.arrive(k_b, passing.at[1])
    add_into(passing.at[1], left[1])
    k_f = links.send(passing.at[1], halves(landing.at[1], 1), to_left)
    yield
    links.arrive(k_c, halves(landing.at[0], 1))
    links.arrive(k_d, halves(landing.at[1], 0))
    links.arrive(k_e, halves(landing.at[0], 0))
    links.arrive(k_f, halves(landing.at[1], 1))
    add_into(own, landing.at[0], landing.at[1])


def reduce_small(links, axis, acc, own, passing, landing):
    right, left = acc(1), acc(-1)
    yield from reduce_axis(
        links,
        axis,
        acc(2),
        (right, halves(right, 0)),
        (left, halves(left, 1)),
        own,
        passing,
        landing,
    )


def rope_rows(position, freqs):
    angles = position.astype(jnp.float32) * freqs
    lane = lax.broadcasted_iota(jnp.int32, angles.shape, 1)
    sine = jnp.sin(angles)
    return jnp.cos(angles), jnp.where(lane < HEAD // 2, -sine, sine)


def swap(values):
    return pltpu.roll(values, HEAD // 2, 1)


def packed_layout(lengths):
    down = lax.broadcasted_iota(jnp.int32, (TOK, 1), 0)
    across = lax.broadcasted_iota(jnp.int32, (1, TOK), 1)
    seg_down = jnp.zeros((TOK, 1), jnp.int32)
    seg_across = jnp.zeros((1, TOK), jnp.int32)
    start = jnp.zeros((TOK, 1), jnp.int32)
    end = 0
    for k in range(SEQS - 1):
        length = lengths[0, k]
        end = end + length
        past = down >= end
        seg_down = seg_down + jnp.where(past, 1, 0)
        seg_across = seg_across + jnp.where(across >= end, 1, 0)
        start = start + jnp.where(past, length, 0)
    allowed = (seg_down == seg_across) & (across <= down)
    return down - start, allowed


def lanes_of(columns, rows):
    lane = lax.broadcasted_iota(jnp.int32, (rows, 128), 1)
    out = jnp.zeros((rows, 128), jnp.float32)
    for k, column in enumerate(columns):
        out = jnp.where(lane == k, column, out)
    return out


def start_sums(links, columns, sums, landing):
    sums[...] = lanes_of(columns, TOK).T[: sums.shape[0]]
    return [links.send(sums, landing.at[k], links.peer(Y, k + 1)) for k in range(3)]


def end_sums(links, sent, sums, landing):
    total = sums[...]
    for k in range(3):
        links.arrive(sent[k], landing.at[k])
        total = total + landing[k]
    fill = jnp.zeros((128 - total.shape[0], TOK), jnp.float32)
    return jnp.concatenate([total, fill], axis=0).T


def front_kernel(
    cuts,
    cot_cuts,
    lengths,
    blocks,
    tokens,
    attn_norm,
    q_gain,
    k_gain,
    ffn_norm,
    router,
    ids,
    freqs,
    cot,
    all_weights,
    rows_out,
    cot_out,
    normed,
    heads,
    raw,
    stats,
    lse,
    mixed,
    resid,
    probs_out,
    weights,
    sums,
    sums_in,
    parts,
    passing,
    landing,
    shard,
    send_sems,
    recv_sems,
    local_sems,
):
    f32, bf16 = jnp.float32, jnp.bfloat16
    links = Links((X, Z, Y), send_sems, recv_sems, pair=True, extra=[(Y, 2)])
    x, z, y = links.at
    core = links.core
    own_block = pltpu.make_async_copy(blocks, weights.at[x, z, core], local_sems.at[0])
    own_block.start()
    half_cols = blocks.shape[1] // 2
    given = []

    def view(cols, places, half):
        index = tuple(places.get(axis, slice(None)) for axis in (X, Z))
        n = blocks.shape[0] // 2
        cut = slice(None) if half is None else pl.ds(half * n, n)
        return weights.at[index + (core, cut, cols)]

    def forward(src, dst):
        given.append((links.send(src, dst, links.pair()), dst))

    gathers = [
        gather_part(
            links,
            functools.partial(view, pl.ds(part * half_cols, half_cols)),
            blocks.at[:, pl.ds(part * half_cols, half_cols)],
            order,
            forward,
        )
        for part, order in enumerate(((X, Z), (Z, X)))
    ]
    for gather in gathers:
        next(gather)

    quarter = TOK // RING

    def rows_view(out, cols, places, half):
        index = tuple(places.get(axis, slice(None)) for axis in (X, Z, Y))
        n = quarter // 2
        cut = slice(None) if half is None else pl.ds(half * n, n)
        return out.at[index + (cut, cols)]

    def row_gathers(out, source, cuts, late):
        return [
            gather_part(
                links,
                functools.partial(rows_view, out, pl.ds(start, size)),
                source.at[:, pl.ds(start, size)],
                order,
                late=order[2] in late,
            )
            for (start, size), order in zip(cuts, ((X, Z, Y), (Z, Y, X), (Y, X, Z)))
        ]

    cot_mine = cot.at[pl.ds(pl.multiple_of(y * quarter, quarter), quarter)]
    cot_here = pltpu.make_async_copy(cot_mine, cot_out.at[x, z, y], local_sems.at[2])
    cot_here.start()
    cot_gathers = row_gathers(cot_out, cot_mine, cot_cuts, (X, Z, Y))
    for gather in cot_gathers:
        next(gather)
    hidden = tokens[...].astype(f32)
    attn_inv = lax.rsqrt(jnp.mean(hidden * hidden, axis=-1, keepdims=True) + EPSILON)
    normed[...] = (hidden * attn_inv * attn_norm[...]).astype(bf16)
    position, allowed = packed_layout(lengths)
    cosine, sine = rope_rows(position, freqs[...])
    cot_here.wait()
    for _ in range(6):
        for gather in gathers + cot_gathers:
            next(gather, None)
    run_all(gathers)
    for k, dst in given:
        links.arrive(k, dst)
    own_block.wait()
    for gather in cot_gathers[1:]:
        next(gather)
    save = pltpu.make_async_copy(weights, all_weights, local_sems.at[0])
    save.start()

    cols = q_gain.shape[1]
    width = tokens.shape[1]

    def project(j):
        w = weights[:, :, :, :, j * cols : (j + 1) * cols].reshape(width, cols)
        return dot(normed[...], w, NN)

    squares = []
    for j in range(2):
        value = project(j)
        raw[:, j * cols : (j + 1) * cols] = value
        squares.append(jnp.sum(value * value, axis=-1, keepdims=True))
    sent = start_sums(links, squares, sums, sums_in)
    heads[:, 2 * cols :] = project(2).astype(bf16)
    total = end_sums(links, sent, sums, sums_in)
    inverse = lax.rsqrt(total / (HEADS * HEAD) + EPSILON)
    stats[...] = inverse
    top_sums = []
    for h in range(cols // HEAD):
        own = slice(h * HEAD, (h + 1) * HEAD)
        rotated = []
        for j, gain in enumerate((q_gain, k_gain)):
            part = raw[:, j * cols + h * HEAD : j * cols + (h + 1) * HEAD]
            part = part * inverse[:, j : j + 1] * gain[:, own]
            part = (part * cosine + swap(part) * sine).astype(bf16)
            heads[:, j * cols + h * HEAD : j * cols + (h + 1) * HEAD] = part
            rotated.append(part)
        scores = dot(rotated[0], rotated[1], NT) * HEAD ** (-0.5)
        scores = jnp.where(allowed, scores, -1e30)
        top = jnp.max(scores, axis=-1, keepdims=True)
        log_total = top + jnp.log(jnp.sum(jnp.exp(scores - top), axis=-1, keepdims=True))
        top_sums.append(log_total)
        probs = jnp.exp(scores - log_total).astype(bf16)
        value = heads[:, 2 * cols + h * HEAD : 2 * cols + (h + 1) * HEAD]
        mixed[:, own] = dot(probs, value, NN).astype(bf16)
    lse[...] = lanes_of(top_sums, TOK)

    out_w = weights[:, :, :, :, 3 * cols :].reshape(width, cols)
    def quarter_rows(step):
        return pl.ds(pl.multiple_of(links.rel(Y, step) * quarter, quarter), quarter)

    for k, step in enumerate((2, 1, -1)):
        parts[k] = dot(mixed[quarter_rows(step), :], out_w, NT).astype(bf16)
    by_step = {2: parts.at[0], 1: parts.at[1], -1: parts.at[2]}
    summing = reduce_small(links, Y, by_step.get, resid, passing, landing)
    next(summing)
    rows = quarter_rows(0)
    resid[...] = tokens[rows, :].astype(f32) + dot(mixed[rows, :], out_w, NT)
    run_all([summing])
    total = resid[...]
    ffn_inv = lax.rsqrt(jnp.mean(total * total, axis=-1, keepdims=True) + EPSILON)
    moe_in = (total * ffn_inv * ffn_norm[...]).astype(bf16)
    logits = dot(moe_in, router[...], NN)
    logits = logits - jnp.max(logits, axis=-1, keepdims=True)
    chances = jnp.exp(logits)
    chances = chances / jnp.sum(chances, axis=-1, keepdims=True)
    mine = ids[rows, :]
    expert = lax.broadcasted_iota(jnp.int32, chances.shape, 1)
    picks = jnp.zeros(chances.shape, f32)
    for k in range(ids.shape[1]):
        picks = picks + jnp.where(mine[:, k : k + 1] == expert, 1.0, 0.0)
    both = jnp.concatenate([chances, picks], axis=1)
    probs_out[...] = both
    shard[:, :width] = moe_in
    shard[:, width:] = both.astype(bf16)
    here = pltpu.make_async_copy(shard, rows_out.at[x, z, y], local_sems.at[1])
    here.start()

    gathers = row_gathers(rows_out, shard, cuts, ())
    last_y, others = cot_gathers[0], cot_gathers[1:]

    def step(parts, count=1):
        for _ in range(count):
            for part in parts:
                next(part, None)

    step(gathers)
    here.wait()
    step(others, 2)
    step([last_y])
    step(gathers, 6)
    step(others)
    step([last_y], 2)
    step(gathers, 2)
    run_all([last_y] + others + gathers)
    save.wait()
    links.close()


def front(
    lengths, blocks, tokens, attn_norm, q_gain, k_gain, ffn_norm, router, ids, cot, collective_id
):
    bf16, f32 = jnp.bfloat16, jnp.float32
    block_rows, wide = blocks.shape
    rows, width = tokens.shape
    cols = q_gain.shape[1]
    quarter = rows // RING
    ext = width + 128
    half = HEAD // 2
    freqs = 10000.0 ** (-jnp.arange(half, dtype=f32) / half)
    freqs = jnp.concatenate([freqs, freqs])[None, :]
    in_vmem = pl.BlockSpec(memory_space=pltpu.VMEM)
    in_hbm = pl.BlockSpec(memory_space=pltpu.HBM)
    shape = jax.ShapeDtypeStruct
    return pl.pallas_call(
        functools.partial(front_kernel, cut_as(4, 6, 7), cut_as(4, 6, 6)),
        in_specs=[pl.BlockSpec(memory_space=pltpu.SMEM), in_hbm] + [in_vmem] * 8 + [in_hbm],
        out_specs=[in_hbm, in_hbm, in_hbm] + [in_vmem] * 8,
        out_shape=[
            shape((RING, RING, 2, block_rows, wide), bf16),
            shape((RING, RING, RING, quarter, ext), bf16),
            shape((RING, RING, RING, quarter, width), bf16),
            shape((rows, width), bf16),
            shape((rows, 3 * cols), bf16),
            shape((rows, 2 * cols), f32),
            shape((rows, 128), f32),
            shape((rows, 128), f32),
            shape((rows, cols), bf16),
            shape((quarter, width), f32),
            shape((quarter, 128), f32),
        ],
        scratch_shapes=[
            pltpu.VMEM((RING, RING, 2, block_rows, wide), bf16),
            pltpu.VMEM((8, rows), f32),
            pltpu.VMEM((3, 8, rows), f32),
            pltpu.VMEM((3, quarter, width), bf16),
            pltpu.VMEM((2, quarter // 2, width), bf16),
            pltpu.VMEM((2, quarter, width), bf16),
            pltpu.VMEM((quarter, ext), bf16),
            pltpu.SemaphoreType.DMA((282,)),
            pltpu.SemaphoreType.DMA((282,)),
            pltpu.SemaphoreType.DMA((3,)),
        ],
        compiler_params=pltpu.CompilerParams(
            collective_id=collective_id, has_side_effects=True, vmem_limit_bytes=VMEM_LIMIT
        ),
        cost_estimate=pl.CostEstimate(flops=0, bytes_accessed=0, transcendentals=0),
        name="front",
    )(lengths, blocks, tokens, attn_norm, q_gain, k_gain, ffn_norm, router, ids, freqs, cot)


ORDER = (2, 1, -1, 0)


def far_first(i):
    return 2 - i + 3 * (i * (i - 1) // 2)


PLAN = {
    (1, 0): (
        (0, 0, 0, 0, 0),
        (0, 1, 0, 0, 0),
        (0, 0, 1, 0, 0),
        (0, 1, 0, 1, 0),
    ),
    (2, 0): (
        (0, 2, 0, 0, 0),
        (0, 0, 2, 0, 0),
        (0, 0, 3, 0, 0),
        (0, 1, 0, 1, 1),
        (0, 2, 0, 1, 0),
        (0, 2, 0, 1, 1),
    ),
    (2, 1): (
        (0, 1, 0, 2, 0),
        (0, 1, 0, 2, 1),
    ),
    (3, 0): (
        (0, 1, 0, 3, 0),
        (0, 1, 0, 3, 1),
        (0, 1, 1, 0, 0),
        (0, 0, 0, 1, 0),
        (0, 0, 0, 2, 0),
        (0, 2, 0, 2, 0),
        (0, 2, 0, 2, 1),
        (0, 0, 1, 1, 0),
        (0, 0, 1, 2, 0),
        (0, 1, 1, 1, 0),
    ),
    (3, 1): (
        (0, 0, 0, 3, 0),
        (0, 2, 0, 3, 0),
        (0, 2, 0, 3, 1),
        (0, 0, 1, 3, 0),
    ),
    (4, 0): (
        (0, 1, 0, 4, 0),
        (0, 2, 1, 0, 0),
        (0, 1, 1, 1, 1),
        (0, 2, 1, 1, 0),
        (0, 2, 1, 1, 1),
        (0, 0, 2, 1, 0),
        (0, 0, 3, 1, 0),
    ),
    (4, 1): (
        (0, 1, 0, 5, 0),
        (1, 1, 0, 0, 0),
        (0, 2, 0, 4, 0),
        (0, 1, 1, 2, 0),
        (0, 1, 1, 2, 1),
    ),
    (5, 0): (
        (0, 2, 0, 5, 0),
        (1, 2, 0, 0, 0),
        (0, 2, 1, 2, 0),
        (0, 2, 1, 2, 1),
        (0, 0, 2, 2, 0),
        (0, 1, 1, 3, 0),
        (0, 0, 3, 2, 0),
        (0, 1, 1, 3, 1),
        (0, 1, 2, 0, 0),
        (0, 0, 0, 1, 1),
        (0, 0, 0, 2, 1),
        (0, 0, 1, 1, 1),
        (0, 0, 1, 2, 1),
        (0, 1, 2, 1, 0),
    ),
    (5, 1): (
        (0, 0, 0, 3, 1),
        (0, 0, 1, 3, 1),
        (0, 2, 1, 3, 0),
        (0, 2, 1, 3, 1),
        (0, 0, 2, 3, 0),
        (0, 0, 3, 3, 0),
    ),
    (6, 0): (
        (0, 1, 1, 4, 0),
        (0, 2, 2, 0, 0),
        (0, 0, 2, 1, 1),
        (0, 1, 2, 1, 1),
        (0, 2, 2, 1, 0),
        (0, 2, 2, 1, 1),
        (0, 0, 3, 1, 1),
    ),
    (6, 1): (
        (0, 1, 1, 5, 0),
        (0, 2, 1, 4, 0),
        (1, 1, 0, 3, 0),
        (0, 1, 2, 2, 0),
        (0, 1, 2, 2, 1),
    ),
    (7, 0): (
        (0, 2, 1, 5, 0),
        (1, 2, 0, 3, 0),
        (0, 0, 0, 4, 0),
        (0, 0, 2, 2, 1),
        (0, 2, 2, 2, 0),
        (0, 2, 2, 2, 1),
        (0, 1, 2, 3, 0),
        (0, 1, 2, 3, 1),
        (0, 1, 3, 0, 0),
        (0, 1, 3, 1, 0),
    ),
    (7, 1): (
        (0, 0, 0, 5, 0),
        (1, 0, 0, 0, 0),
        (0, 0, 1, 4, 0),
        (0, 0, 3, 2, 1),
        (0, 0, 2, 3, 1),
        (0, 2, 2, 3, 0),
        (0, 2, 2, 3, 1),
    ),
    (8, 0): (
        (0, 0, 1, 5, 0),
        (0, 1, 2, 4, 0),
        (0, 0, 3, 3, 1),
        (0, 2, 3, 0, 0),
        (0, 1, 3, 1, 1),
        (0, 2, 3, 1, 0),
        (0, 2, 3, 1, 1),
        (0, 1, 2, 5, 0),
        (1, 1, 0, 3, 1),
        (0, 1, 3, 2, 0),
        (0, 1, 3, 2, 1),
        (0, 2, 2, 4, 0),
        (0, 1, 3, 3, 0),
        (0, 1, 3, 3, 1),
        (0, 0, 2, 4, 0),
        (0, 2, 2, 5, 0),
        (1, 2, 0, 3, 1),
        (0, 0, 2, 5, 0),
        (1, 0, 0, 3, 1),
        (3, 0, 0, 0, 0),
        (0, 0, 3, 4, 0),
        (0, 2, 3, 2, 0),
        (0, 2, 3, 2, 1),
        (3, 0, 0, 0, 0),
        (0, 0, 3, 5, 0),
        (0, 2, 3, 3, 0),
        (0, 2, 3, 3, 1),
        (1, 0, 0, 3, 0),
        (3, 0, 0, 0, 0),
        (3, 0, 0, 0, 0),
        (0, 1, 3, 4, 0),
        (3, 0, 0, 0, 0),
        (0, 1, 3, 5, 0),
        (1, 1, 0, 5, 0),
        (2, 1, 0, 0, 0),
        (3, 0, 0, 0, 0),
        (0, 2, 3, 4, 0),
        (2, 1, 0, 3, 0),
        (2, 1, 0, 3, 1),
        (0, 2, 3, 5, 0),
        (1, 0, 0, 5, 0),
        (2, 0, 0, 0, 0),
        (3, 0, 0, 0, 0),
        (2, 1, 0, 5, 0),
        (2, 0, 0, 3, 0),
        (2, 0, 0, 3, 1),
        (3, 0, 0, 0, 0),
        (1, 2, 0, 5, 0),
        (2, 2, 0, 0, 0),
        (2, 0, 0, 5, 0),
        (3, 0, 0, 0, 0),
        (2, 2, 0, 3, 0),
        (2, 2, 0, 3, 1),
        (3, 0, 0, 0, 0),
        (3, 0, 0, 0, 0),
        (2, 2, 0, 5, 0),
    ),
}


class RingSum:
    def __init__(self, links, axis, term, passed, landed, side, stage, own, final, sems, before):
        self.links, self.axis, self.term = links, axis, term
        self.passed, self.landed, self.side, self.stage = passed, landed, side, stage
        self.own, self.final, self.sems, self.before = own, final, sems, before
        self.k = {(n, d): links.reserve() for n in ("pass", "direct", "sum") for d in (0, 1)}

    def first(self):
        for d, step in enumerate((1, -1)):
            self.links.send(
                functools.partial(self.term, 2, d),
                functools.partial(self.passed, d),
                self.links.peer(self.axis, step),
                self.k["pass", d],
            )

    def direct(self, d):
        step = (1, -1)[d]
        self.links.send(
            functools.partial(self.term, step, 1 - d),
            lambda: halves(self.landed(d), 1 - d),
            self.links.peer(self.axis, step),
            self.k["direct", d],
        )

    def side_load(self, d):
        return pltpu.make_async_copy(
            self.term((1, -1)[d], d), self.side.at[d], self.sems.at[d]
        )

    def stage_load(self, d):
        return pltpu.make_async_copy(self.passed(d), self.stage.at[d], self.sems.at[2 + d])

    def prepare(self, d):
        self.side_load(d).start()
        if self.before is not None:
            self.links.sent(self.before.k["sum", d], self.stage.at[d])
        self.links.arrive(self.k["pass", d], self.passed(d))
        self.stage_load(d).start()

    def onward(self, d):
        self.side_load(d).wait()
        self.stage_load(d).wait()
        add_into(self.stage.at[d], self.side.at[d])
        self.links.send(
            lambda: self.stage.at[d],
            lambda: halves(self.landed(d), d),
            self.links.peer(self.axis, (1, -1)[d]),
            self.k["sum", d],
        )

    def own_load(self):
        return pltpu.make_async_copy(self.term(0, None), self.own, self.sems.at[4])

    def final_load(self, d):
        return pltpu.make_async_copy(self.landed(d), self.final.at[d], self.sems.at[5 + d])

    def collect(self):
        self.own_load().start()
        for d in (0, 1):
            self.links.arrive(self.k["direct", d], halves(self.landed(d), 1 - d))
            self.links.arrive(self.k["sum", d], halves(self.landed(d), d))
            self.final_load(d).start()

    def finish(self):
        self.own_load().wait()
        for d in (0, 1):
            self.final_load(d).wait()
        add_into(self.own, self.final.at[0], self.final.at[1])


class NearSum:
    def __init__(self, links, axis, acc, passing, landing):
        self.links, self.axis, self.acc = links, axis, acc
        self.passing, self.landing = passing, landing
        self.k = {(n, d): links.reserve() for n in ("pass", "direct", "sum") for d in (0, 1)}

    def first(self):
        for d, step in enumerate((1, -1)):
            self.links.send(
                lambda d=d: halves(self.acc(2), d),
                lambda d=d: self.passing.at[d],
                self.links.peer(self.axis, step),
                self.k["pass", d],
            )

    def onward(self, d):
        step = (1, -1)[d]
        peer = self.links.peer(self.axis, step)
        self.links.send(
            lambda: halves(self.acc(step), 1 - d),
            lambda: halves(self.landing.at[d], 1 - d),
            peer,
            self.k["direct", d],
        )
        self.links.arrive(self.k["pass", d], self.passing.at[d])
        add_into(self.passing.at[d], halves(self.acc(step), d))
        self.links.send(
            lambda: self.passing.at[d],
            lambda: halves(self.landing.at[d], d),
            peer,
            self.k["sum", d],
        )

    def finish(self):
        for d in (0, 1):
            self.links.arrive(self.k["direct", d], halves(self.landing.at[d], 1 - d))
            self.links.arrive(self.k["sum", d], halves(self.landing.at[d], d))
        add_into(self.acc(0), self.landing.at[0], self.landing.at[1])


def experts_kernel(
    cuts,
    x_all,
    dy_all,
    w_own,
    w_pair,
    resid,
    chances,
    router,
    ffn_norm,
    cot,
    d_resid,
    out_mine,
    d_resid_mine,
    small_rows,
    grad_experts,
    grad_down,
    xs,
    ds,
    act,
    ret,
    pair_in,
    *refs,
):
    f32, bf16 = jnp.float32, jnp.bfloat16
    hbm, refs = refs[:6], refs[6:]
    bufs, refs = refs[:27], refs[27:]
    (
        home,
        stage,
        cot_now,
        send_sems,
        recv_sems,
        ring_sems,
        load_sems,
        store_sems,
        weight_sems,
        cot_sem,
        grad_load_sems,
        grad_pair_sems,
        grad_store_sems,
    ) = refs
    links = Links((X, Z, Y), send_sems, recv_sems, pair=True)
    here_x, here_z, here_y = links.at
    rows = ret.shape[3]
    width = resid.shape[1]
    ff = act.shape[2] // 3
    cap = CAP
    locals_ = xs.shape[0]
    half_experts = locals_ // 2
    group = (here_x * RING + here_z) * 2
    ids = [(group + links.core) * half_experts + j for j in range(half_experts)]
    ids += [(group + 1 - links.core) * half_experts + j for j in range(half_experts)]

    cot_rows = cot.at[pl.ds(pl.multiple_of(here_y * rows, rows), rows)]
    cot_load = pltpu.make_async_copy(cot_rows, cot_now, cot_sem)
    cot_load.start()

    def group_at(s, g):
        gx = lax.rem(here_x + far_first(s // 2) + RING, RING)
        gz = lax.rem(here_z + far_first(2 * (s % 2) + g) + RING, RING)
        return gx, gz

    orders = ((X, Z, Y), (Z, X, Y), (Y, X, Z))
    far, near, last = [], [], []
    for p, ((start, size), (a1, a2, a3)) in enumerate(zip(cuts, orders)):
        side, stg, acc, final, pass_b, land_b, pass_c, land_c, _ = bufs[9 * p : 9 * p + 9]
        passed, landed = hbm[2 * p : 2 * p + 2]

        def term(a1, a2, c, start, size, step, half):
            places = {a1: links.rel(a1, step), a2: links.rel(a2, ORDER[c])}
            index = tuple(places.get(axis, slice(None)) for axis in (X, Z, Y))
            cut = slice(None) if half is None else pl.ds(half * (rows // 2), rows // 2)
            return ret.at[index + (cut, pl.ds(start, size))]

        slots = side.shape[0]
        chunks = []
        for c in range(4):
            chunks.append(
                RingSum(
                    links,
                    a1,
                    functools.partial(term, a1, a2, c, start, size),
                    lambda d, passed=passed, c=c: passed.at[d, c],
                    lambda d, landed=landed, c=c: landed.at[d, c],
                    side.at[c % slots],
                    stg.at[c % slots],
                    acc.at[c],
                    final,
                    ring_sems.at[p, c],
                    chunks[c - slots] if c >= slots else None,
                )
            )
        far.append(chunks)
        near.append(
            NearSum(links, a2, lambda step, acc=acc: acc.at[ORDER.index(step)], pass_b, land_b)
        )
        last.append(
            NearSum(
                links,
                a3,
                lambda step, acc=acc, a3=a3: acc.at[3, links.rel(a3, step)],
                pass_c,
                land_c,
            )
        )

    rings = (far, near, last)

    def act_at(key, work=None):
        for kind, p, c, method, d in PLAN.get(key, ()):
            if kind == 3:
                next(work, None)
                continue
            ring = far[p][c] if kind == 0 else rings[kind][p]
            name = ("first", "direct", "prepare", "onward", "collect", "finish")[method]
            call = getattr(ring, name)
            call(d) if method in (1, 2, 3) else call()

    lane = lax.broadcasted_iota(jnp.int32, (2 * locals_, 128), 1)
    row = lax.broadcasted_iota(jnp.int32, (2 * locals_, 128), 0)
    select = jnp.zeros((2 * locals_, 128), f32)
    for j in range(locals_):
        select = jnp.where((row == j) & (lane == ids[j] + EXPERTS), 1.0, select)
        select = jnp.where((row == locals_ + j) & (lane == ids[j]), 1.0, select)
    select = select.astype(bf16)
    before = jnp.where(
        lax.broadcasted_iota(jnp.int32, (TOK, TOK), 0)
        < lax.broadcasted_iota(jnp.int32, (TOK, TOK), 1),
        1.0,
        0.0,
    ).astype(bf16)
    slots = lax.broadcasted_iota(jnp.int32, (cap, TOK), 0).astype(f32)
    out_lane = lax.broadcasted_iota(jnp.int32, (2 * cap, 128), 1)
    def groups(weights, x, dy, xs_now, ds_now, act_now, terms, ret_now):
        def weight_loads():
            return [
                pltpu.make_async_copy(w_own, weights.at[0], weight_sems.at[0]),
                pltpu.make_async_copy(w_pair, weights.at[1], weight_sems.at[1]),
            ]

        for copy in weight_loads():
            copy.start()

        def loads(s):
            copies = []
            for g in range(2):
                gx, gz = group_at(s, g)
                copies.append(pltpu.make_async_copy(x_all.at[gx, gz], x.at[g], load_sems.at[g, 0]))
                copies.append(pltpu.make_async_copy(dy_all.at[gx, gz], dy.at[g], load_sems.at[g, 1]))
            return copies

        def rows_of(s):
            start = s * 2 * cap
            return pl.ds(start if isinstance(s, int) else pl.multiple_of(start, 2 * cap), 2 * cap)

        def row_stores(s):
            at = rows_of(s)
            return [
                pltpu.make_async_copy(xs_now, xs.at[:, at], store_sems.at[0]),
                pltpu.make_async_copy(ds_now, ds.at[:, at], store_sems.at[1]),
            ]

        def act_store(s):
            at = rows_of(s)
            return pltpu.make_async_copy(act_now, act.at[:, at], store_sems.at[2])

        def ret_store(s, g):
            gx, gz = group_at(s, g)
            return pltpu.make_async_copy(ret_now.at[g], ret.at[gx, gz], store_sems.at[3 + g])

        for copy in loads(0):
            copy.start()

        @pl.loop(0, 8)
        def _(s):
            places, gates = [], []
            for copy in loads(s):
                copy.wait()

            @pl.when(s > 0)
            def _():
                for copy in row_stores(s):
                    copy.wait()

            for g in range(2):
                marks = x[g, :, :, width:].reshape(TOK, 128)
                flags = dot(select, marks, NT)
                slot = dot(flags.astype(bf16), before, NN)
                place, gate = [], []
                for j in range(locals_):
                    hit = (slots == slot[j : j + 1]) & (flags[j : j + 1] > 0.5)
                    place.append(jnp.where(hit, 1.0, 0.0))
                    gate.append(
                        jnp.sum(place[-1] * flags[locals_ + j : locals_ + j + 1], axis=1, keepdims=True)
                    )
                place = jnp.concatenate(place, axis=0).astype(bf16)
                places.append(place)
                gates.append(gate)
                picked = dot(place, x[g, :, :, :width].reshape(TOK, width), NN).astype(bf16)
                picked_dy = dot(place, dy[g].reshape(TOK, width), NN).astype(bf16)
                for j in range(locals_):
                    xs_now[j, g * cap : (g + 1) * cap, :] = picked[j * cap : (j + 1) * cap]
                    ds_now[j, g * cap : (g + 1) * cap, :] = picked_dy[j * cap : (j + 1) * cap]
            for copy in row_stores(s):
                copy.start()

            @pl.when(s < 7)
            def _():
                for copy in loads(s + 1):
                    copy.start()

            @pl.when(s == 0)
            def _():
                for copy in weight_loads():
                    copy.wait()

            @pl.when(s > 0)
            def _():
                act_store(s).wait()
                for g in range(2):
                    ret_store(s, g).wait()

            for k in range(1, 8):
                pl.when(s == k)(functools.partial(act_at, (k, 0)))

            for j in range(locals_):
                if j == half_experts:
                    for k in range(1, 8):
                        pl.when(s == k)(functools.partial(act_at, (k, 1)))
                w = weights.at[j // half_experts, j % half_experts]
                gate = jnp.concatenate([gates[g][j] for g in range(2)], axis=0)
                up_in = dot(xs_now[j], w[0], NN)
                up = dot(xs_now[j], w[1], NN)
                d_raw = dot(ds_now[j], w[2], NN)
                sig = 1.0 / (1.0 + jnp.exp(-up_in))
                silu = up_in * sig
                hidden = (silu * up).astype(bf16).astype(f32)
                d_gate = jnp.sum(hidden * d_raw, axis=1, keepdims=True)
                gated = (hidden * gate).astype(bf16)
                d_hidden = d_raw * gate
                d_up_in = (d_hidden * up * sig * (1.0 + up_in * (1.0 - sig))).astype(bf16)
                d_up = (d_hidden * silu).astype(bf16)
                act_now[j, :, :ff] = gated
                act_now[j, :, ff : 2 * ff] = d_up_in
                act_now[j, :, 2 * ff :] = d_up
                y = dot(gated, w[2], NT).astype(bf16)
                dx = (dot(d_up_in, w[0], NT) + dot(d_up, w[1], NT)).astype(bf16)
                dg = jnp.where(out_lane == ids[j], d_gate, 0.0).astype(bf16)
                for g in range(2):
                    part = slice(g * cap, (g + 1) * cap)
                    there = slice(j * cap, (j + 1) * cap)
                    terms[g, there, :width] = y[part]
                    terms[g, there, width : 2 * width] = dx[part]
                    terms[g, there, 2 * width :] = dg[part]
            act_store(s).start()
            for g in range(2):
                for start, size in cuts:
                    cut = slice(start, start + size)
                    ret_now[g, :, :, cut] = (
                        dot(places[g], terms[g, :, cut], TN).astype(bf16).reshape(RING, rows, size)
                    )
                ret_store(s, g).start()

        for g in range(2):
            ret_store(0, g).wait()
        for copy in row_stores(0) + [act_store(0)]:
            copy.wait()

    wide = x_all.shape[4]
    pl.run_scoped(
        groups,
        pltpu.VMEM((2,) + w_own.shape, bf16),
        pltpu.VMEM((2, RING, rows, wide), bf16),
        pltpu.VMEM((2, RING, rows, width), bf16),
        pltpu.VMEM((locals_, 2 * cap, width), bf16),
        pltpu.VMEM((locals_, 2 * cap, width), bf16),
        pltpu.VMEM((locals_, 2 * cap, 3 * ff), bf16),
        pltpu.VMEM((2, locals_ * cap, ret.shape[4]), bf16),
        pltpu.VMEM((2, RING, rows, ret.shape[4]), bf16),
    )

    def ending(xs_e, ds_e, act_e, given, taken, summed):
        def loads(j):
            e = (j + half_experts) % locals_
            return [
                pltpu.make_async_copy(src.at[e], dst.at[j % 2], grad_load_sems.at[j % 2, i])
                for i, (src, dst) in enumerate(((xs, xs_e), (ds, ds_e), (act, act_e)))
            ]

        def take(n):
            return pltpu.make_async_copy(
                pair_in.at[n // 3, n % 3], taken.at[n % 2], grad_pair_sems.at[n % 2]
            )

        def store(n):
            e, i = n // 3, n % 3
            dst = grad_down.at[e] if i == 2 else grad_experts.at[e, i]
            return pltpu.make_async_copy(summed.at[n % 2], dst, grad_store_sems.at[n % 2])

        sent = []

        def work():
            for copy in loads(0):
                copy.start()
            for j in range(locals_):
                for copy in loads(j):
                    copy.wait()
                if j + 1 < locals_:
                    for copy in loads(j + 1):
                        copy.start()
                for i in range(3):
                    rows_in = ds_e if i == 2 else xs_e
                    cols_in = (slice(ff, 2 * ff), slice(2 * ff, 3 * ff), slice(0, ff))[i]
                    n = (j % half_experts) * 3 + i
                    own = j >= half_experts
                    if own:
                        links.arrive(sent[n], pair_in.at[n // 3, n % 3])
                        take(n).start()
                        if n >= 2:
                            store(n - 2).wait()
                        take(n).wait()

                    @pl.loop(0, RING)
                    def _(q):
                        cut = pl.ds(pl.multiple_of(q * (width // RING), width // RING), width // RING)
                        part = dot(rows_in[j % 2, :, cut], act_e[j % 2, :, cols_in], TN)
                        if own:
                            summed[n % 2, cut, :] = part + taken[n % 2, cut, :].astype(f32)
                        else:
                            given[n, cut, :] = part.astype(bf16)

                    if own:
                        store(n).start()
                    else:
                        sent.append(
                            links.send(given.at[n], pair_in.at[n // 3, n % 3], links.pair())
                        )
                    yield

        piece = work()
        act_at((8, 0), piece)
        go_on()
        for _ in piece:
            pass
        for n in (3 * half_experts - 2, 3 * half_experts - 1):
            store(n).wait()
        for k in sent:
            links.sent(k, given.at[0])
        links.close()

    def go_on():
        for p, (start, size) in enumerate(cuts):
            acc = bufs[9 * p + 2]
            home[:, start : start + size] = acc[3, links.at[orders[p][2]]]
        cot_load.wait()

        values = resid[...]
        inverse = lax.rsqrt(jnp.mean(values * values, axis=-1, keepdims=True) + EPSILON)
        hat = values * inverse
        moe_in = (hat * ffn_norm[...]).astype(bf16)
        probs, picks = chances[:, :EXPERTS], chances[:, EXPERTS:]
        d_probs = home[:, 2 * width : 2 * width + EXPERTS].astype(f32) * picks
        d_logits = probs * (d_probs - jnp.sum(probs * d_probs, axis=-1, keepdims=True))
        d_logits = d_logits.astype(bf16)
        d_moe = home[:, width : 2 * width].astype(f32) + dot(d_logits, router[...], NT)
        d_hat = d_moe * ffn_norm[...]
        final = cot_now[...].astype(f32) + inverse * (
            d_hat - hat * jnp.mean(d_hat * hat, axis=-1, keepdims=True)
        )
        d_resid_mine[...] = final
        stage[...] = final.astype(bf16)
        here = pl.ds(pl.multiple_of(here_y * rows, rows), rows)
        copy = pltpu.make_async_copy(stage, d_resid.at[here], cot_sem)
        copy.start()

        def view(places, half):
            start = places[Y] * rows + (0 if half is None else half * (rows // 2))
            size = rows if half is None else rows // 2
            return d_resid.at[pl.ds(pl.multiple_of(start, size), size)]

        sharing = gather_part(links, view, stage, (Y,))
        next(sharing)
        out_mine[...] = (values + home[:, :width].astype(f32)).astype(bf16)
        small_rows[:EXPERTS, :] = dot(d_logits, moe_in, TN)
        row = lax.broadcasted_iota(jnp.int32, (8, width), 0)
        d_ffn = jnp.sum(d_moe * hat, axis=0, keepdims=True)
        small_rows[EXPERTS:, :] = jnp.where(row == 1, d_ffn, 0.0)
        run_all([sharing])
        copy.wait()

    chunk = xs.shape[1:]
    pl.run_scoped(
        ending,
        pltpu.VMEM((2,) + chunk, bf16),
        pltpu.VMEM((2,) + chunk, bf16),
        pltpu.VMEM((2,) + act.shape[1:], bf16),
        pltpu.VMEM((3 * half_experts, width, ff), bf16),
        pltpu.VMEM((2, width, ff), bf16),
        pltpu.VMEM((2, width, ff), f32),
    )


def experts(x_all, dy_all, w_own, w_pair, resid, chances, router, ffn_norm, cot, collective_id):
    rows, wide = x_all.shape[3:]
    width = dy_all.shape[4]
    ff = w_own.shape[3]
    locals_ = 2 * w_own.shape[0]
    groups = RING * RING
    bf16, f32 = jnp.bfloat16, jnp.float32
    cols = 2 * width + 128
    cuts = cut_as(9, 11, 13)
    vmem, dma = pltpu.VMEM, pltpu.SemaphoreType.DMA
    bufs, hbm_out = [], []
    shape = jax.ShapeDtypeStruct
    for p, (_, size) in enumerate(cuts):
        slots = 2 if p == 0 else 1
        hbm_out += [
            shape((2, 4, RING, rows // 2, size), bf16),
            shape((2, 4, RING, rows, size), bf16),
        ]
        bufs += [
            vmem((slots, 2, RING, rows // 2, size), bf16),
            vmem((slots, 2, RING, rows // 2, size), bf16),
            vmem((4, RING, rows, size), bf16),
            vmem((2, RING, rows, size), bf16),
            vmem((2, RING, rows // 2, size), bf16),
            vmem((2, RING, rows, size), bf16),
            vmem((2, rows // 2, size), bf16),
            vmem((2, rows, size), bf16),
            vmem((8, 128), bf16),
        ]
    in_vmem = pl.BlockSpec(memory_space=vmem)
    in_hbm = pl.BlockSpec(memory_space=pltpu.HBM)
    return pl.pallas_call(
        functools.partial(experts_kernel, cuts),
        in_specs=[in_hbm] * 4 + [in_vmem] * 4 + [in_hbm],
        out_specs=[in_hbm] + [in_vmem] * 3 + [in_hbm] * 13,
        out_shape=[
            shape((RING * rows, width), bf16),
            shape((rows, width), bf16),
            shape((rows, width), f32),
            shape((EXPERTS + 8, width), f32),
            shape((locals_ // 2, 2, width, ff), f32),
            shape((locals_ // 2, width, ff), f32),
            shape((locals_, groups * CAP, width), bf16),
            shape((locals_, groups * CAP, width), bf16),
            shape((locals_, groups * CAP, 3 * ff), bf16),
            shape((RING, RING, RING, rows, cols), bf16),
            shape((locals_ // 2, 3, width, ff), bf16),
        ]
        + hbm_out,
        scratch_shapes=bufs
        + [
            vmem((rows, cols), bf16),
            vmem((rows, width), bf16),
            vmem((rows, width), bf16),
            dma((118,)),
            dma((118,)),
            dma((3, 4, 7)),
            dma((2, 2)),
            dma((5,)),
            dma((2,)),
            dma,
            dma((2, 3)),
            dma((2,)),
            dma((2,)),
        ],
        compiler_params=pltpu.CompilerParams(
            collective_id=collective_id, has_side_effects=True, vmem_limit_bytes=VMEM_LIMIT
        ),
        cost_estimate=pl.CostEstimate(flops=0, bytes_accessed=0, transcendentals=0),
        name="experts",
    )(x_all, dy_all, w_own, w_pair, resid, chances, router, ffn_norm, cot)


def reduce_plane_part(links, order, region, pair_in, bufs):
    pass_a, land_a, pass_b, land_b = bufs
    a1, a2 = order
    steps = (2, 1, -1, 0)
    given = []
    for i, step in enumerate(steps):
        places = {a1: links.rel(a1, step)}
        src = region(places, 1 - links.core)
        given.append(links.send(src, pair_in.at[i], links.pair()))
    yield
    mine = {}
    for i, step in enumerate(steps):
        mine[step] = region({a1: links.rel(a1, step)}, links.core)
        links.arrive(given[i], pair_in.at[i])
        add_into(mine[step], pair_in.at[i])
    yield from reduce_small(links, a1, lambda step: mine[step], mine[0], pass_a, land_a)
    yield

    def at(step):
        return region({a1: links.at[a1], a2: links.rel(a2, step)}, links.core)

    yield from reduce_small(links, a2, at, at(0), pass_b, land_b)


def plane_buffers(rows, size):
    return [
        pltpu.VMEM(shape, jnp.bfloat16)
        for shape in (
            (4, RING, rows, size),
            (2, RING, rows // 2, size),
            (2, RING, rows, size),
            (2, rows // 2, size),
            (2, rows, size),
        )
    ]


def back_kernel(
    lengths,
    d_resid,
    weights,
    heads,
    raw,
    stats,
    lse,
    mixed,
    normed,
    tokens,
    attn_norm,
    q_gain,
    k_gain,
    d_resid_mine,
    small_rows,
    out_mine,
    freqs,
    input_grad,
    out,
    grad_qkv,
    grad_out,
    grad_router,
    grad_attn,
    grad_ffn,
    grad_q,
    grad_k,
    terms,
    d_mixed,
    d_rot,
    d_proj,
    sums,
    sums_in,
    parts,
    passing,
    landing,
    d_normed,
    grads_in,
    rows_small,
    held,
    small_in,
    *rest,
):
    f32, bf16 = jnp.float32, jnp.bfloat16
    bufs, (send_sems, recv_sems, local_sem) = rest[:-3], rest[-3:]
    links = Links((X, Z, Y), send_sems, recv_sems, pair=True, extra=[(Y, 2), (X, 2), (Z, 2)])
    x, z, y = links.at
    core = links.core
    cols = q_gain.shape[1]
    rows, width = tokens.shape
    quarter = rows // RING
    block_rows = terms.shape[3]
    mine = pl.ds(pl.multiple_of(y * quarter, quarter), quarter)
    out_here = pltpu.make_async_copy(out_mine, out.at[mine], local_sem)
    out_here.start()

    def out_view(places, half):
        size = quarter if half is None else quarter // 2
        start = places[Y] * quarter + (half or 0) * size
        return out.at[pl.ds(pl.multiple_of(start, size), size)]

    out_sharing = gather_part(links, out_view, out_mine, (Y,))
    position, allowed = packed_layout(lengths)
    cosine, sine = rope_rows(position, freqs[...])
    scale = HEAD ** (-0.5)

    def weight(start, stop):
        return weights[:, :, :, :, start:stop].reshape(width, stop - start)

    d_mixed[...] = dot(d_resid[...], weight(3 * cols, 4 * cols), NN).astype(bf16)
    rows_small[...] = jnp.zeros(rows_small.shape, f32)
    rows_small[: small_rows.shape[0], :] = small_rows[...]
    means = [jnp.zeros((rows, 1), f32), jnp.zeros((rows, 1), f32)]
    for h in range(cols // HEAD):
        own = slice(h * HEAD, (h + 1) * HEAD)
        query, key, value = (
            heads[:, j * cols + h * HEAD : j * cols + (h + 1) * HEAD] for j in range(3)
        )
        scores = dot(query, key, NT) * scale
        probs = jnp.exp(jnp.where(allowed, scores, -1e30) - lse[:, h : h + 1])
        probs = jnp.where(allowed, probs, 0.0)
        d_out = d_mixed[:, own]
        d_proj[:, 2 * cols + h * HEAD : 2 * cols + (h + 1) * HEAD] = dot(
            probs.astype(bf16), d_out, TN
        ).astype(bf16)
        d_probs = dot(d_out, value, NT)
        d_scores = probs * (d_probs - jnp.sum(probs * d_probs, axis=-1, keepdims=True))
        d_scores = d_scores.astype(bf16)
        turned = (dot(d_scores, key, NN) * scale, dot(d_scores, query, TN) * scale)
        for j, (grad, gain) in enumerate(zip(turned, (q_gain, k_gain))):
            at = slice(j * cols + h * HEAD, j * cols + (h + 1) * HEAD)
            grad = grad * cosine - swap(grad) * sine
            hat = raw[:, at] * stats[:, j : j + 1]
            place_at = pl.ds(pl.multiple_of(y * cols + h * HEAD, HEAD), HEAD)
            rows_small[66 + j : 67 + j, place_at] = jnp.sum(grad * hat, axis=0, keepdims=True)
            grad = grad * gain[:, own]
            d_rot[:, at] = grad
            means[j] = means[j] + jnp.sum(grad * hat, axis=-1, keepdims=True)
    sent = start_sums(links, means, sums, sums_in)

    def fill(left, right, start):
        size = right.shape[1]

        @pl.loop(0, RING)
        def _(i):
            block = 2 * RING * block_rows
            some = left[:, pl.ds(pl.multiple_of(i * block, block), block)]
            terms[i, :, :, :, start : start + size] = (
                dot(some, right, TN).astype(bf16).reshape(RING, 2, block_rows, size)
            )

    def region(cut, places, at_core):
        index = tuple(places.get(axis, slice(None)) for axis in (X, Z))
        return terms.at[index + (at_core, slice(None), cut)]

    def reduction(part, start, size, order):
        own = bufs[5 * part : 5 * part + 5]
        cut = pl.ds(start, size)
        return reduce_plane_part(links, order, functools.partial(region, cut), own[0], own[1:])

    fill(normed, d_proj[:, 2 * cols :], 2 * cols)
    fill(d_resid, mixed[...], 3 * cols)
    first = reduction(0, 2 * cols, 2 * cols, (X, Z))
    next(first)
    total = end_sums(links, sent, sums, sums_in) / (HEADS * HEAD)
    for j in range(2):
        at = slice(j * cols, (j + 1) * cols)
        inverse = stats[:, j : j + 1]
        hat = raw[:, at] * inverse
        d_proj[:, at] = (inverse * (d_rot[:, at] - hat * total[:, j : j + 1])).astype(bf16)
    next(first)
    proj = weight(0, 3 * cols)

    def quarter_rows(step):
        return pl.ds(pl.multiple_of(links.rel(Y, step) * quarter, quarter), quarter)

    for k, step in enumerate((2, 1, -1)):
        parts[k] = dot(d_proj[quarter_rows(step), :], proj, NT).astype(bf16)
    by_step = {2: parts.at[0], 1: parts.at[1], -1: parts.at[2]}
    summing = reduce_small(links, Y, by_step.get, d_normed, passing, landing)
    next(summing)
    d_normed[...] = dot(d_proj[mine, :], proj, NT)
    fill(normed, d_proj[:, : 2 * cols], 0)
    second = reduction(1, 0, 2 * cols, (Z, X))
    next(second)
    next(summing)
    next(first)
    run_all([summing])
    hidden = tokens[mine, :].astype(f32)
    inverse = lax.rsqrt(jnp.mean(hidden * hidden, axis=-1, keepdims=True) + EPSILON)
    hat = hidden * inverse
    rows_small[64:65, :] = jnp.sum(d_normed[...] * hat, axis=0, keepdims=True)
    d_hat = d_normed[...] * attn_norm[...]
    final = d_resid_mine[...] + inverse * (
        d_hat - hat * jnp.mean(d_hat * hat, axis=-1, keepdims=True)
    )
    grads_in[y] = final.astype(bf16)

    def grads_view(places, half):
        if half is None:
            return grads_in.at[places[Y]]
        return grads_in.at[places[Y], pl.ds(half * (quarter // 2), quarter // 2)]

    sharing = gather_part(links, grads_view, grads_in.at[y], (Y,))
    next(sharing)
    next(out_sharing)
    wide = 4 * cols
    terms[:, :, :, :, wide:] = (
        rows_small[...].T.astype(bf16).reshape(RING, RING, 2, block_rows, rows_small.shape[0])
    )
    third = reduction(2, wide, rows_small.shape[0], (X, Z))
    next(third)
    next(second)
    next(first, None)
    next(second, None)
    run_all([third, first, second, sharing, out_sharing])

    here = terms.at[x, z, core]
    small = here.at[:, pl.ds(wide, rows_small.shape[0])]
    sent = [links.send(small, small_in.at[k], links.peer(Y, k + 1)) for k in range(3)]
    for j in range(3):
        grad_qkv[j] = here[:, j * cols : (j + 1) * cols].astype(f32)
    grad_out[...] = here[:, 3 * cols : 4 * cols].astype(f32)
    total = small[...].astype(f32)
    for k in range(3):
        links.arrive(sent[k], small_in.at[k])
        total = total + small_in[k].astype(f32)
    held[x, z, core] = total.astype(bf16)
    own = held.at[x, z, core]
    sent = [links.send(own, own, links.peer(X, step)) for step in (2, 1, -1)]
    for q in range(RING):
        input_grad[q * quarter : (q + 1) * quarter, :] = grads_in[q].astype(f32)
    for k, step in zip(sent, (2, 1, -1)):
        links.arrive(k, held.at[links.rel(X, -step), z, core])
    own = held.at[:, z, core]
    sent = [links.send(own, own, links.peer(Z, step)) for step in (2, 1, -1)]
    for k, step in zip(sent, (2, 1, -1)):
        links.arrive(k, held.at[:, links.rel(Z, -step), core])
    own = held.at[:, :, core]
    k = links.send(own, own, links.pair())
    links.arrive(k, held.at[:, :, 1 - core])
    total = held[...].astype(f32).reshape(width, rows_small.shape[0])
    grad_router[...] = total[:, :EXPERTS]
    rows_small[...] = total.T
    grad_attn[...] = rows_small[64:65, :]
    grad_ffn[...] = rows_small[65:66, :]
    out_here.wait()
    cut = pl.ds(pl.multiple_of(y * cols, cols), cols)
    grad_q[...] = rows_small[66:67, cut]
    grad_k[...] = rows_small[67:68, cut]
    links.close()


def back(
    lengths,
    d_resid,
    weights,
    heads,
    raw,
    stats,
    lse,
    mixed,
    normed,
    tokens,
    attn_norm,
    q_gain,
    k_gain,
    d_resid_mine,
    small_rows,
    out_mine,
    collective_id,
):
    bf16, f32 = jnp.bfloat16, jnp.float32
    rows, width = tokens.shape
    cols = q_gain.shape[1]
    quarter = rows // RING
    block_rows = weights.shape[3]
    half = HEAD // 2
    freqs = 10000.0 ** (-jnp.arange(half, dtype=f32) / half)
    freqs = jnp.concatenate([freqs, freqs])[None, :]
    in_vmem = pl.BlockSpec(memory_space=pltpu.VMEM)
    shape = jax.ShapeDtypeStruct
    vmem = pltpu.VMEM
    buffers = []
    for size in (2 * cols, 2 * cols, 128):
        buffers += plane_buffers(block_rows, size)
    return pl.pallas_call(
        back_kernel,
        in_specs=[pl.BlockSpec(memory_space=pltpu.SMEM)] + [in_vmem] * 16,
        out_specs=[in_vmem, pl.BlockSpec(memory_space=pltpu.HBM)] + [in_vmem] * 7,
        out_shape=[
            shape((rows, width), f32),
            shape((rows, width), bf16),
            shape((3, block_rows, cols), f32),
            shape((block_rows, cols), f32),
            shape((width, EXPERTS), f32),
            shape((1, width), f32),
            shape((1, width), f32),
            shape((1, cols), f32),
            shape((1, cols), f32),
        ],
        scratch_shapes=[
            vmem((RING, RING, 2, block_rows, 4 * cols + 128), bf16),
            vmem((rows, cols), bf16),
            vmem((rows, 2 * cols), f32),
            vmem((rows, 3 * cols), bf16),
            vmem((8, rows), f32),
            vmem((3, 8, rows), f32),
            vmem((3, quarter, width), bf16),
            vmem((2, quarter // 2, width), bf16),
            vmem((2, quarter, width), bf16),
            vmem((quarter, width), f32),
            vmem((RING, quarter, width), bf16),
            vmem((128, width), f32),
            vmem((RING, RING, 2, block_rows, 128), bf16),
            vmem((3, block_rows, 128), bf16),
        ]
        + buffers
        + [
            pltpu.SemaphoreType.DMA((80,)),
            pltpu.SemaphoreType.DMA((80,)),
            pltpu.SemaphoreType.DMA,
        ],
        compiler_params=pltpu.CompilerParams(
            collective_id=collective_id, has_side_effects=True, vmem_limit_bytes=VMEM_LIMIT
        ),
        cost_estimate=pl.CostEstimate(flops=0, bytes_accessed=0, transcendentals=0),
        name="back",
    )(
        lengths,
        d_resid,
        weights,
        heads,
        raw,
        stats,
        lse,
        mixed,
        normed,
        tokens,
        attn_norm,
        q_gain,
        k_gain,
        d_resid_mine,
        small_rows,
        out_mine,
        freqs,
    )


def body(
    tokens,
    attn_norm,
    qkv_weights,
    out_weight,
    q_gain,
    k_gain,
    ffn_norm,
    router,
    expert_weights,
    lengths,
    expert_ids,
    cotangent,
):
    blocks = jnp.concatenate([qkv_weights[0], qkv_weights[1], qkv_weights[2], out_weight], axis=1)
    pairs = [(i, i ^ 1) for i in range(lax.axis_size("expert"))]
    pair_weights = lax.ppermute(expert_weights, "expert", pairs)
    all_weights, rows_all, cot_rows, normed_b, heads, raw, inverses, lse, mixed_b, resid, chances = front(
        lengths,
        blocks,
        tokens,
        attn_norm[None],
        q_gain[None],
        k_gain[None],
        ffn_norm[None],
        router,
        expert_ids,
        cotangent,
        1,
    )
    d_resid, out_mine, d_resid_mine, small_rows, grad_experts, grad_down = experts(
        rows_all,
        cot_rows,
        expert_weights,
        pair_weights,
        resid,
        chances,
        router,
        ffn_norm[None],
        cotangent,
        3,
    )[:6]
    input_grad, output, grad_qkv, grad_out, grad_router, grad_attn, grad_ffn, grad_q, grad_k = back(
        lengths,
        d_resid,
        all_weights,
        heads,
        raw,
        inverses,
        lse,
        mixed_b,
        normed_b,
        tokens,
        attn_norm[None],
        q_gain[None],
        k_gain[None],
        d_resid_mine,
        small_rows,
        out_mine,
        4,
    )
    return (
        output,
        input_grad,
        grad_attn[0],
        grad_qkv,
        grad_out,
        grad_q[0],
        grad_k[0],
        grad_ffn[0],
        grad_router,
        grad_experts,
        grad_down,
    )


def solution(mesh):
    placed = (
        P(("dp", "expert"), None),
        P(),
        P(None, ("dp", "expert"), "mp"),
        P(("dp", "expert"), "mp"),
        P("mp"),
        P("mp"),
        P(),
        P(),
        P(("dp", "expert"), None, None, "mp"),
        P(("dp", "expert"), None),
        P(("dp", "expert"), None),
        P(("dp", "expert"), None),
    )
    return jax.shard_map(
        body,
        mesh=mesh,
        in_specs=placed,
        out_specs=(
            P(("dp", "expert"), None),
            P(("dp", "expert"), None),
            P(),
            P(None, ("dp", "expert"), "mp"),
            P(("dp", "expert"), "mp"),
            P("mp"),
            P("mp"),
            P(),
            P(),
            P(("dp", "expert"), None, None, "mp"),
            P(("dp", "expert"), None, "mp"),
        ),
        check_vma=False,
    )
```

```python
import functools

import jax
import jax.numpy as jnp
from jax import lax
from jax.experimental import pallas as pl
from jax.experimental.pallas import tpu as pltpu
from jax.sharding import PartitionSpec as P

HEADS = 16
HEAD = 128
TOK = 256
SEQS = 4
EXPERTS = 64
CAP = 48
VMEM_LIMIT = 63000000


EPSILON = 1e-05


def dot(a, b, dims):
    return lax.dot_general(a, b, (dims, ((), ())), preferred_element_type=jnp.float32)


NN = ((1,), (0,))
NT = ((1,), (1,))
TN = ((0,), (0,))


RING = 4
X, Z, Y = 0, 1, 2


def place():
    x, e, y = (lax.axis_index(name) for name in ("dp", "expert", "mp"))
    return (x, e // 2, y), e % 2


def device_at(axis, at, core):
    return {X: {"dp": at}, Z: {"expert": at * 2 + core}, Y: {"mp": at}}[axis]


class Links:
    def __init__(self, axes, send_sems, recv_sems, pair=False, extra=()):
        self.at, self.core = place()
        self.send_sems, self.recv_sems, self.used, self.open = send_sems, recv_sems, 0, {}
        self.ended = set()
        barrier = pltpu.get_barrier_semaphore()
        peers = [self.peer(axis, step) for axis in axes for step in (1, -1)]
        peers += [self.peer(axis, step) for axis, step in extra]
        if pair:
            peers.append(self.pair())
        for peer in peers:
            pl.semaphore_signal(
                barrier, inc=1, device_id=peer, device_id_type=pl.DeviceIdType.MESH
            )
        pl.semaphore_wait(barrier, len(peers))

    def rel(self, axis, step):
        return lax.rem(self.at[axis] + (step + RING), RING)

    def peer(self, axis, step):
        return device_at(axis, self.rel(axis, step), self.core)

    def pair(self):
        return {"expert": self.at[Z] * 2 + (1 - self.core)}

    def copy(self, k, src, dst, peer):
        return pltpu.make_async_remote_copy(
            src_ref=src,
            dst_ref=dst,
            send_sem=self.send_sems.at[k],
            recv_sem=self.recv_sems.at[k],
            device_id=peer,
            device_id_type=pl.DeviceIdType.MESH,
        )

    def reserve(self):
        k = self.used
        assert k < self.send_sems.shape[0]
        self.used += 1
        return k

    def send(self, src, dst, peer, k=None):
        k = self.reserve() if k is None else k
        dst = dst() if callable(dst) else dst
        self.copy(k, src() if callable(src) else src, dst, peer).start()
        self.open[k] = src
        return k

    def sent(self, k, src):
        src = src() if callable(src) else src
        self.copy(k, src, src, self.pair()).wait_send()
        self.ended.add(k)

    def arrive(self, k, dst):
        self.copy(k, dst, dst, self.pair()).wait_recv()

    def close(self):
        for k, src in self.open.items():
            if k not in self.ended:
                self.sent(k, src)


def run_all(steps):
    steps = list(steps)
    while steps:
        steps = [s for s in steps if next(s, "end") != "end"]


def gather_part(links, view, shard, order, forward=None, late=False):
    mine = [links.at[axis] for axis in order]
    n = len(order)
    arrived = [{} for _ in order]
    held = []

    def region(i, c, step, half=None):
        places = {}
        for j, axis in enumerate(order):
            if j == i:
                places[axis] = links.rel(axis, step)
            elif j > i:
                places[axis] = mine[j]
            elif j == i - 1 and c is not None:
                places[axis] = links.rel(axis, c)
        return view(places, half)

    def own(i, c):
        if late and i == n - 1 and c not in held:
            held.append(c)
            return
        src = shard if i == 0 or (i == 1 and c == 0) else region(i, c, 0)
        for step in (1, -1):
            k = links.send(src, region(i, c, 0), links.peer(order[i], step))
            arrived[i][c, -step] = k

    def onward(i, c, step):
        links.arrive(arrived[i][c, step], region(i, c, step))
        half = 0 if step == -1 else 1
        part = region(i, c, step, half)
        arrived[i][c, 2, half] = links.send(part, part, links.peer(order[i], -step))

    def opposite(i, c):
        for half in (0, 1):
            links.arrive(arrived[i][c, 2, half], region(i, c, 2, half))

    for i in range(n):
        chunks = [None] if i == 0 else [0, -1, 1, 2]
        if late and i == n - 1:
            for c in chunks:
                own(i, c)
            yield
        if i == 0:
            own(0, None)
            if forward:
                forward(shard, region(0, None, 0))
            if n > 1:
                own(1, 0)
            yield
        for step in (-1, 1):
            for c in chunks:
                onward(i, c, step)
            if i + 1 < n:
                own(i + 1, step)
            if forward:
                forward(region(i, None, step), region(i, None, step))
            yield
        for c in chunks:
            opposite(i, c)
        if i + 1 < n:
            own(i + 1, 2)
        if i + 2 < n:
            own(i + 2, 0)
        if forward:
            forward(region(i, None, 2), region(i, None, 2))
        yield


def cut_as(*tiles):
    return [(sum(tiles[:i]) * 128, size * 128) for i, size in enumerate(tiles)]


def add_into(dst, *others):
    def one(d, *refs):
        total = d[...].astype(jnp.float32)
        for ref in refs:
            total = total + ref[...].astype(jnp.float32)
        d[...] = total.astype(d.dtype)

    if len(dst.shape) == 2:
        one(dst, *others)
    else:

        @pl.loop(0, dst.shape[0])
        def _(i):
            one(dst.at[i], *(ref.at[i] for ref in others))


def halves(ref, half):
    rows = ref.shape[-2]
    cut = pl.ds(half * (rows // 2), rows // 2)
    return ref.at[cut] if len(ref.shape) == 2 else ref.at[:, cut]


def reduce_axis(links, axis, opp, right, left, own, passing, landing, ready=None):
    to_right, to_left = links.peer(axis, 1), links.peer(axis, -1)
    k_a = links.send(halves(opp, 0), passing.at[0], to_right)
    k_b = links.send(halves(opp, 1), passing.at[1], to_left)
    k_c = links.send(halves(right[0], 1), halves(landing.at[0], 1), to_right)
    k_d = links.send(halves(left[0], 0), halves(landing.at[1], 0), to_left)
    yield
    if ready is not None:
        ready()
    links.arrive(k_a, passing.at[0])
    add_into(passing.at[0], right[1])
    k_e = links.send(passing.at[0], halves(landing.at[0], 0), to_right)
    links.arrive(k_b, passing.at[1])
    add_into(passing.at[1], left[1])
    k_f = links.send(passing.at[1], halves(landing.at[1], 1), to_left)
    yield
    links.arrive(k_c, halves(landing.at[0], 1))
    links.arrive(k_d, halves(landing.at[1], 0))
    links.arrive(k_e, halves(landing.at[0], 0))
    links.arrive(k_f, halves(landing.at[1], 1))
    add_into(own, landing.at[0], landing.at[1])


def reduce_small(links, axis, acc, own, passing, landing):
    right, left = acc(1), acc(-1)
    yield from reduce_axis(
        links,
        axis,
        acc(2),
        (right, halves(right, 0)),
        (left, halves(left, 1)),
        own,
        passing,
        landing,
    )


def rope_rows(position, freqs):
    angles = position.astype(jnp.float32) * freqs
    lane = lax.broadcasted_iota(jnp.int32, angles.shape, 1)
    sine = jnp.sin(angles)
    return jnp.cos(angles), jnp.where(lane < HEAD // 2, -sine, sine)


def swap(values):
    return pltpu.roll(values, HEAD // 2, 1)


def packed_layout(lengths):
    down = lax.broadcasted_iota(jnp.int32, (TOK, 1), 0)
    across = lax.broadcasted_iota(jnp.int32, (1, TOK), 1)
    seg_down = jnp.zeros((TOK, 1), jnp.int32)
    seg_across = jnp.zeros((1, TOK), jnp.int32)
    start = jnp.zeros((TOK, 1), jnp.int32)
    end = 0
    for k in range(SEQS - 1):
        length = lengths[0, k]
        end = end + length
        past = down >= end
        seg_down = seg_down + jnp.where(past, 1, 0)
        seg_across = seg_across + jnp.where(across >= end, 1, 0)
        start = start + jnp.where(past, length, 0)
    allowed = (seg_down == seg_across) & (across <= down)
    return down - start, allowed


def lanes_of(columns, rows):
    lane = lax.broadcasted_iota(jnp.int32, (rows, 128), 1)
    out = jnp.zeros((rows, 128), jnp.float32)
    for k, column in enumerate(columns):
        out = jnp.where(lane == k, column, out)
    return out


def start_sums(links, columns, sums, landing):
    sums[...] = lanes_of(columns, TOK).T[: sums.shape[0]]
    return [links.send(sums, landing.at[k], links.peer(Y, k + 1)) for k in range(3)]


def end_sums(links, sent, sums, landing):
    total = sums[...]
    for k in range(3):
        links.arrive(sent[k], landing.at[k])
        total = total + landing[k]
    fill = jnp.zeros((128 - total.shape[0], TOK), jnp.float32)
    return jnp.concatenate([total, fill], axis=0).T


FRONT = (
    (
        0, 1, 2, 3, 1, 3, 0, 1, 4, 0, 1, 1, 0, 0, 2, 4, 3, 1, 3, 4, 2, 0, 2, 3, 2, 4, 4,
    ),
    (
        4, 3, 4, 3,
    ),
    (),
    (),
    (),
    (),
    (),
    (
        6, 7, 4, 4, 5, 7, 3, 6, 2, 7, 5, 5, 6, 3, 2, 7, 7, 4, 7, 6, 6, 6, 5, 3, 7, 6, 2,
        2, 5, 5, 7, 7, 2, 5, 6, 6, 5, 5, 7, 6, 5,
    ),
)


def front_kernel(
    cuts,
    cot_cuts,
    lengths,
    qkv,
    out_weight,
    tokens,
    attn_norm,
    q_gain,
    k_gain,
    ffn_norm,
    router,
    ids,
    freqs,
    cot,
    all_weights,
    rows_out,
    cot_out,
    normed,
    heads,
    raw,
    stats,
    lse,
    mixed,
    resid,
    probs_out,
    weights,
    sums,
    sums_in,
    parts,
    passing,
    landing,
    shard,
    chosen,
    blocks,
    whole,
    send_sems,
    recv_sems,
    local_sems,
):
    f32, bf16 = jnp.float32, jnp.bfloat16
    cols = q_gain.shape[1]
    pieces = [
        pltpu.make_async_copy(
            qkv.at[j] if j < 3 else out_weight,
            blocks.at[:, pl.ds(j * cols, cols)],
            local_sems.at[3 + j],
        )
        for j in range(4)
    ]
    for piece in pieces:
        piece.start()
    links = Links((X, Z, Y), send_sems, recv_sems, pair=True, extra=[(Y, 2)])
    for piece in pieces:
        piece.wait()
    x, z, y = links.at
    core = links.core
    own_block = pltpu.make_async_copy(blocks, weights.at[x, z, core], local_sems.at[0])
    own_block.start()
    half_cols = blocks.shape[1] // 2
    given = []

    def view(cols, places, half):
        index = tuple(places.get(axis, slice(None)) for axis in (X, Z))
        n = blocks.shape[0] // 2
        cut = slice(None) if half is None else pl.ds(half * n, n)
        return weights.at[index + (core, cut, cols)]

    def forward(src, dst):
        given.append((links.send(src, dst, links.pair()), dst))

    gathers = [
        gather_part(
            links,
            functools.partial(view, pl.ds(part * half_cols, half_cols)),
            blocks.at[:, pl.ds(part * half_cols, half_cols)],
            order,
            forward,
        )
        for part, order in enumerate(((X, Z), (Z, X)))
    ]
    for gather in gathers:
        next(gather)

    quarter = TOK // RING

    def rows_view(out, cols, places, half):
        index = tuple(places.get(axis, slice(None)) for axis in (X, Z, Y))
        n = quarter // 2
        cut = slice(None) if half is None else pl.ds(half * n, n)
        return out.at[index + (cut, cols)]

    def row_gathers(out, source, cuts, late):
        return [
            gather_part(
                links,
                functools.partial(rows_view, out, pl.ds(start, size)),
                source.at[:, pl.ds(start, size)],
                order,
                late=order[2] in late,
            )
            for (start, size), order in zip(cuts, ((X, Z, Y), (Z, Y, X), (Y, X, Z)))
        ]

    cot_mine = cot.at[pl.ds(pl.multiple_of(y * quarter, quarter), quarter)]
    cot_here = pltpu.make_async_copy(cot_mine, cot_out.at[x, z, y], local_sems.at[2])
    cot_here.start()
    cot_gathers = row_gathers(cot_out, cot_mine, cot_cuts, (X, Z, Y))
    for gather in cot_gathers:
        next(gather)
    parts_of = gathers + cot_gathers

    def steps(segment):
        for part in FRONT[segment]:
            next(parts_of[part], None)

    hidden = tokens[...].astype(f32)
    attn_inv = lax.rsqrt(jnp.mean(hidden * hidden, axis=-1, keepdims=True) + EPSILON)
    normed[...] = (hidden * attn_inv * attn_norm[...]).astype(bf16)
    position, allowed = packed_layout(lengths)
    cosine, sine = rope_rows(position, freqs[...])
    expert = lax.broadcasted_iota(jnp.int32, (128, TOK), 0)
    picks = jnp.zeros((128, TOK), f32)
    for k in range(ids.shape[0]):
        picks = picks + jnp.where(ids[k : k + 1, :] == expert, 1.0, 0.0)
    chosen[...] = picks.T
    cot_here.wait()
    steps(0)
    run_all(gathers)
    for k, dst in given:
        links.arrive(k, dst)
    own_block.wait()
    save = pltpu.make_async_copy(weights, all_weights, local_sems.at[0])
    save.start()

    width = tokens.shape[1]

    def project(j):
        w = weights[:, :, :, :, j * cols : (j + 1) * cols].reshape(width, cols)
        return dot(normed[...], w, NN)

    squares = []
    for j in range(2):
        value = project(j)
        raw[:, j * cols : (j + 1) * cols] = value
        squares.append(jnp.sum(value * value, axis=-1, keepdims=True))
    sent = start_sums(links, squares, sums, sums_in)
    heads[:, 2 * cols :] = project(2).astype(bf16)
    steps(1)
    total = end_sums(links, sent, sums, sums_in)
    inverse = lax.rsqrt(total / (HEADS * HEAD) + EPSILON)
    stats[...] = inverse
    top_sums = []
    for h in range(cols // HEAD):
        own = slice(h * HEAD, (h + 1) * HEAD)
        rotated = []
        for j, gain in enumerate((q_gain, k_gain)):
            part = raw[:, j * cols + h * HEAD : j * cols + (h + 1) * HEAD]
            part = part * inverse[:, j : j + 1] * gain[:, own]
            part = (part * cosine + swap(part) * sine).astype(bf16)
            heads[:, j * cols + h * HEAD : j * cols + (h + 1) * HEAD] = part
            rotated.append(part)
        steps(2 + h)
        scores = dot(rotated[0], rotated[1], NT) * HEAD ** (-0.5)
        scores = jnp.where(allowed, scores, -1e30)
        top = jnp.max(scores, axis=-1, keepdims=True)
        log_total = top + jnp.log(jnp.sum(jnp.exp(scores - top), axis=-1, keepdims=True))
        top_sums.append(log_total)
        probs = jnp.exp(scores - log_total).astype(bf16)
        value = heads[:, 2 * cols + h * HEAD : 2 * cols + (h + 1) * HEAD]
        mixed[:, own] = dot(probs, value, NN).astype(bf16)
    lse[...] = lanes_of(top_sums, TOK)
    steps(6)
    out_w = weights[:, :, :, :, 3 * cols :].reshape(width, cols)
    def quarter_rows(step):
        return pl.ds(pl.multiple_of(links.rel(Y, step) * quarter, quarter), quarter)

    whole[...] = dot(mixed[...], out_w, NT)
    for k, step in enumerate((2, 1, -1)):
        parts[k] = whole[quarter_rows(step), :].astype(bf16)
    by_step = {2: parts.at[0], 1: parts.at[1], -1: parts.at[2]}
    summing = reduce_small(links, Y, by_step.get, resid, passing, landing)
    next(summing)
    rows = quarter_rows(0)
    resid[...] = tokens[rows, :].astype(f32) + whole[rows, :]
    run_all([summing])
    total = resid[...]
    ffn_inv = lax.rsqrt(jnp.mean(total * total, axis=-1, keepdims=True) + EPSILON)
    moe_in = (total * ffn_inv * ffn_norm[...]).astype(bf16)
    logits = dot(moe_in, router[...], NT)
    logits = logits - jnp.max(logits, axis=-1, keepdims=True)
    chances = jnp.exp(logits)
    chances = chances / jnp.sum(chances, axis=-1, keepdims=True)
    picks = chosen[rows, :EXPERTS]
    both = jnp.concatenate([chances, picks], axis=1)
    probs_out[...] = both
    shard[:, :width] = moe_in
    shard[:, width:] = both.astype(bf16)
    here = pltpu.make_async_copy(shard, rows_out.at[x, z, y], local_sems.at[1])
    here.start()

    parts_of += row_gathers(rows_out, shard, cuts, ())
    seen = set()
    for part in FRONT[7]:
        if part >= 5 and part in seen and here is not None:
            here.wait()
            here = None
        seen.add(part)
        next(parts_of[part], None)
    run_all(parts_of)
    save.wait()
    links.close()


def front(
    lengths,
    qkv,
    out_weight,
    tokens,
    attn_norm,
    q_gain,
    k_gain,
    ffn_norm,
    router,
    ids,
    cot,
    collective_id,
):
    bf16, f32 = jnp.bfloat16, jnp.float32
    rows, width = tokens.shape
    cols = q_gain.shape[1]
    block_rows, wide = out_weight.shape[0], 4 * cols
    quarter = rows // RING
    ext = width + 128
    half = HEAD // 2
    freqs = 10000.0 ** (-jnp.arange(half, dtype=f32) / half)
    freqs = jnp.concatenate([freqs, freqs])[None, :]
    in_vmem = pl.BlockSpec(memory_space=pltpu.VMEM)
    in_hbm = pl.BlockSpec(memory_space=pltpu.HBM)
    shape = jax.ShapeDtypeStruct
    return pl.pallas_call(
        functools.partial(front_kernel, cut_as(4, 6, 7), cut_as(4, 6, 6)),
        in_specs=[pl.BlockSpec(memory_space=pltpu.SMEM)] + [in_hbm] * 2 + [in_vmem] * 8 + [in_hbm],
        out_specs=[in_hbm, in_hbm, in_hbm] + [in_vmem] * 8,
        out_shape=[
            shape((RING, RING, 2, block_rows, wide), bf16),
            shape((RING, RING, RING, quarter, ext), bf16),
            shape((RING, RING, RING, quarter, width), bf16),
            shape((rows, width), bf16),
            shape((rows, 3 * cols), bf16),
            shape((rows, 2 * cols), f32),
            shape((rows, 128), f32),
            shape((rows, 128), f32),
            shape((rows, cols), bf16),
            shape((quarter, width), f32),
            shape((quarter, 128), f32),
        ],
        scratch_shapes=[
            pltpu.VMEM((RING, RING, 2, block_rows, wide), bf16),
            pltpu.VMEM((8, rows), f32),
            pltpu.VMEM((3, 8, rows), f32),
            pltpu.VMEM((3, quarter, width), bf16),
            pltpu.VMEM((2, quarter // 2, width), bf16),
            pltpu.VMEM((2, quarter, width), bf16),
            pltpu.VMEM((quarter, ext), bf16),
            pltpu.VMEM((rows, 128), f32),
            pltpu.VMEM((block_rows, wide), bf16),
            pltpu.VMEM((rows, width), f32),
            pltpu.SemaphoreType.DMA((282,)),
            pltpu.SemaphoreType.DMA((282,)),
            pltpu.SemaphoreType.DMA((7,)),
        ],
        compiler_params=pltpu.CompilerParams(
            collective_id=collective_id, has_side_effects=True, vmem_limit_bytes=VMEM_LIMIT
        ),
        cost_estimate=pl.CostEstimate(flops=0, bytes_accessed=0, transcendentals=0),
        name="front",
    )(
        lengths,
        qkv,
        out_weight,
        tokens,
        attn_norm,
        q_gain,
        k_gain,
        ffn_norm,
        router,
        ids,
        freqs,
        cot,
    )


ORDER = (2, 1, -1, 0)


def far_first(i):
    return 2 - i + 3 * (i * (i - 1) // 2)


ORDERS = ((0, 1, 2), (1, 0, 2), (2, 0, 1))

TILES = (9, 12, 12)

PLAN = {
    (1, 0): (
        (0, 0, 0, 0, 0),
        (0, 1, 0, 0, 0),
        (0, 2, 0, 0, 0),
        (0, 0, 1, 0, 0),
        (0, 0, 2, 0, 0),
        (0, 0, 3, 0, 0),
        (0, 1, 0, 1, 0),
        (0, 1, 0, 1, 1),
        (0, 2, 0, 1, 0),
        (0, 2, 0, 1, 1),
    ),
    (2, 0): (
        (0, 1, 0, 2, 0),
        (0, 1, 0, 2, 1),
        (0, 2, 0, 2, 0),
        (0, 2, 0, 2, 1),
        (0, 1, 1, 0, 0),
        (0, 2, 1, 0, 0),
        (0, 0, 0, 1, 0),
        (0, 0, 0, 2, 0),
        (0, 0, 1, 1, 0),
        (0, 0, 1, 2, 0),
        (0, 1, 1, 1, 0),
        (0, 1, 1, 1, 1),
        (0, 2, 1, 1, 0),
        (0, 2, 1, 1, 1),
        (0, 0, 2, 1, 0),
        (0, 0, 3, 1, 0),
    ),
    (2, 1): (
        (0, 1, 0, 3, 0),
        (0, 0, 0, 3, 0),
        (0, 1, 0, 3, 1),
        (0, 2, 0, 3, 0),
        (0, 2, 0, 3, 1),
        (0, 0, 1, 3, 0),
    ),
    (3, 0): (
        (0, 1, 2, 0, 0),
        (0, 2, 2, 0, 0),
        (0, 0, 0, 1, 1),
        (0, 0, 0, 2, 1),
        (0, 0, 1, 1, 1),
        (0, 0, 1, 2, 1),
        (0, 0, 2, 1, 1),
        (0, 1, 2, 1, 0),
        (0, 1, 2, 1, 1),
        (0, 2, 2, 1, 0),
        (0, 2, 2, 1, 1),
        (0, 0, 3, 1, 1),
    ),
    (3, 2): (
        (0, 1, 0, 4, 0),
        (0, 2, 0, 4, 0),
        (0, 1, 1, 2, 0),
        (0, 1, 1, 2, 1),
        (0, 2, 1, 2, 0),
        (0, 2, 1, 2, 1),
        (0, 0, 0, 3, 1),
        (0, 0, 1, 3, 1),
    ),
    (4, 0): (
        (0, 1, 0, 5, 0),
        (1, 1, 0, 0, 0),
        (0, 2, 0, 5, 0),
        (1, 2, 0, 0, 0),
        (0, 0, 2, 2, 0),
        (0, 1, 1, 3, 0),
        (0, 1, 1, 3, 1),
        (0, 2, 1, 3, 0),
        (0, 2, 1, 3, 1),
        (0, 1, 3, 0, 0),
        (0, 2, 3, 0, 0),
        (0, 1, 3, 1, 0),
        (0, 1, 3, 1, 1),
        (0, 2, 3, 1, 0),
        (0, 2, 3, 1, 1),
        (0, 0, 3, 2, 0),
        (0, 0, 2, 3, 0),
        (0, 0, 3, 3, 0),
        (3, 0, 0, 0, 0),
        (0, 1, 2, 2, 0),
        (0, 1, 2, 2, 1),
        (0, 2, 2, 2, 0),
        (0, 0, 2, 2, 1),
        (0, 1, 2, 3, 0),
        (0, 2, 2, 2, 1),
        (0, 1, 1, 4, 0),
        (0, 1, 2, 3, 1),
        (0, 0, 0, 4, 0),
        (0, 2, 2, 3, 0),
        (0, 2, 1, 4, 0),
        (0, 0, 2, 3, 1),
        (0, 2, 2, 3, 1),
        (0, 1, 1, 5, 0),
        (1, 1, 0, 3, 0),
        (0, 0, 0, 5, 0),
        (1, 0, 0, 0, 0),
        (0, 2, 1, 5, 0),
        (0, 0, 1, 4, 0),
        (0, 0, 3, 2, 1),
        (1, 2, 0, 3, 0),
        (0, 0, 1, 5, 0),
        (0, 0, 3, 3, 1),
        (3, 0, 0, 0, 0),
        (3, 0, 0, 0, 0),
        (3, 0, 0, 0, 0),
        (3, 0, 0, 0, 0),
        (0, 1, 3, 2, 0),
        (0, 1, 3, 2, 1),
        (0, 2, 3, 2, 0),
        (0, 2, 3, 2, 1),
        (0, 1, 3, 3, 0),
        (0, 1, 2, 4, 0),
        (0, 1, 3, 3, 1),
        (0, 2, 3, 3, 0),
        (0, 2, 2, 4, 0),
        (0, 2, 3, 3, 1),
        (0, 1, 2, 5, 0),
        (1, 1, 0, 3, 1),
        (0, 0, 2, 4, 0),
        (0, 2, 2, 5, 0),
        (1, 0, 0, 3, 0),
        (1, 2, 0, 3, 1),
        (0, 0, 2, 5, 0),
        (1, 0, 0, 3, 1),
        (0, 0, 3, 4, 0),
        (3, 0, 0, 0, 0),
        (0, 0, 3, 5, 0),
        (0, 2, 3, 4, 0),
        (0, 1, 3, 4, 0),
        (0, 2, 3, 5, 0),
        (0, 1, 3, 5, 0),
        (3, 0, 0, 0, 0),
        (3, 0, 0, 0, 0),
        (3, 0, 0, 0, 0),
        (1, 0, 0, 5, 0),
        (2, 0, 0, 0, 0),
        (1, 1, 0, 5, 0),
        (2, 1, 0, 0, 0),
        (3, 0, 0, 0, 0),
        (2, 0, 0, 3, 0),
        (2, 0, 0, 3, 1),
        (2, 1, 0, 3, 0),
        (2, 1, 0, 3, 1),
        (3, 0, 0, 0, 0),
        (2, 0, 0, 5, 0),
        (3, 0, 0, 0, 0),
        (2, 1, 0, 5, 0),
        (1, 2, 0, 5, 0),
        (2, 2, 0, 0, 0),
        (2, 2, 0, 3, 0),
        (2, 2, 0, 3, 1),
        (2, 2, 0, 5, 0),
    ),
}


class RingSum:
    def __init__(self, links, axis, term, passed, landed, side, stage, own, final, sems, before):
        self.links, self.axis, self.term = links, axis, term
        self.passed, self.landed, self.side, self.stage = passed, landed, side, stage
        self.own, self.final, self.sems, self.before = own, final, sems, before
        self.k = {(n, d): links.reserve() for n in ("pass", "direct", "sum") for d in (0, 1)}

    def first(self):
        for d, step in enumerate((1, -1)):
            self.links.send(
                functools.partial(self.term, 2, d),
                functools.partial(self.passed, d),
                self.links.peer(self.axis, step),
                self.k["pass", d],
            )

    def direct(self, d):
        step = (1, -1)[d]
        self.links.send(
            functools.partial(self.term, step, 1 - d),
            lambda: halves(self.landed(d), 1 - d),
            self.links.peer(self.axis, step),
            self.k["direct", d],
        )

    def side_load(self, d):
        return pltpu.make_async_copy(
            self.term((1, -1)[d], d), self.side.at[d], self.sems.at[d]
        )

    def stage_load(self, d):
        return pltpu.make_async_copy(self.passed(d), self.stage.at[d], self.sems.at[2 + d])

    def prepare(self, d):
        self.side_load(d).start()
        if self.before is not None:
            self.links.sent(self.before.k["sum", d], self.stage.at[d])
        self.links.arrive(self.k["pass", d], self.passed(d))
        self.stage_load(d).start()

    def onward(self, d):
        self.side_load(d).wait()
        self.stage_load(d).wait()
        add_into(self.stage.at[d], self.side.at[d])
        self.links.send(
            lambda: self.stage.at[d],
            lambda: halves(self.landed(d), d),
            self.links.peer(self.axis, (1, -1)[d]),
            self.k["sum", d],
        )

    def own_load(self):
        return pltpu.make_async_copy(self.term(0, None), self.own, self.sems.at[4])

    def final_load(self, d):
        return pltpu.make_async_copy(self.landed(d), self.final.at[d], self.sems.at[5 + d])

    def collect(self):
        self.own_load().start()
        for d in (0, 1):
            self.links.arrive(self.k["direct", d], halves(self.landed(d), 1 - d))
            self.links.arrive(self.k["sum", d], halves(self.landed(d), d))
            self.final_load(d).start()

    def finish(self):
        self.own_load().wait()
        for d in (0, 1):
            self.final_load(d).wait()
        add_into(self.own, self.final.at[0], self.final.at[1])


class NearSum:
    def __init__(self, links, axis, acc, passing, landing):
        self.links, self.axis, self.acc = links, axis, acc
        self.passing, self.landing = passing, landing
        self.k = {(n, d): links.reserve() for n in ("pass", "direct", "sum") for d in (0, 1)}

    def first(self):
        for d, step in enumerate((1, -1)):
            self.links.send(
                lambda d=d: halves(self.acc(2), d),
                lambda d=d: self.passing.at[d],
                self.links.peer(self.axis, step),
                self.k["pass", d],
            )

    def onward(self, d):
        step = (1, -1)[d]
        peer = self.links.peer(self.axis, step)
        self.links.send(
            lambda: halves(self.acc(step), 1 - d),
            lambda: halves(self.landing.at[d], 1 - d),
            peer,
            self.k["direct", d],
        )
        self.links.arrive(self.k["pass", d], self.passing.at[d])
        add_into(self.passing.at[d], halves(self.acc(step), d))
        self.links.send(
            lambda: self.passing.at[d],
            lambda: halves(self.landing.at[d], d),
            peer,
            self.k["sum", d],
        )

    def finish(self):
        for d in (0, 1):
            self.links.arrive(self.k["direct", d], halves(self.landing.at[d], 1 - d))
            self.links.arrive(self.k["sum", d], halves(self.landing.at[d], d))
        add_into(self.acc(0), self.landing.at[0], self.landing.at[1])


def ring_sums(links, source, cuts, orders, hbm, bufs, ring_sems):
    rows = source.shape[3]
    far, near, last = [], [], []
    for p, ((start, size), (a1, a2, a3)) in enumerate(zip(cuts, orders)):
        side, stg, acc, final, pass_b, land_b, pass_c, land_c = bufs[8 * p : 8 * p + 8]
        passed, landed = hbm[2 * p : 2 * p + 2]

        def term(a1, a2, c, start, size, step, half):
            places = {a1: links.rel(a1, step), a2: links.rel(a2, ORDER[c])}
            index = tuple(places.get(axis, slice(None)) for axis in (X, Z, Y))
            cut = slice(None) if half is None else pl.ds(half * (rows // 2), rows // 2)
            return source.at[index + (cut, pl.ds(start, size))]

        slots = side.shape[0]
        chunks = []
        for c in range(4):
            chunks.append(
                RingSum(
                    links,
                    a1,
                    functools.partial(term, a1, a2, c, start, size),
                    lambda d, passed=passed, c=c: passed.at[d, c],
                    lambda d, landed=landed, c=c: landed.at[d, c],
                    side.at[c % slots],
                    stg.at[c % slots],
                    acc.at[c],
                    final,
                    ring_sems.at[p, c],
                    chunks[c - slots] if c >= slots else None,
                )
            )
        far.append(chunks)
        near.append(
            NearSum(links, a2, lambda step, acc=acc: acc.at[ORDER.index(step)], pass_b, land_b)
        )
        last.append(
            NearSum(
                links,
                a3,
                lambda step, acc=acc, a3=a3: acc.at[3, links.rel(a3, step)],
                pass_c,
                land_c,
            )
        )
    return far, near, last


def act_on(rings, actions, work=None):
    for kind, p, c, method, d in actions:
        if kind == 3:
            next(work, None)
            continue
        ring = rings[0][p][c] if kind == 0 else rings[kind][p]
        name = ("first", "direct", "prepare", "onward", "collect", "finish")[method]
        call = getattr(ring, name)
        call(d) if method in (1, 2, 3) else call()


def ring_buffers(rows, cuts):
    bf16, vmem = jnp.bfloat16, pltpu.VMEM
    landing, buffers = [], []
    for p, (_, size) in enumerate(cuts):
        slots = 2 if p == 0 else 1
        landing += [
            jax.ShapeDtypeStruct((2, 4, RING, rows // 2, size), bf16),
            jax.ShapeDtypeStruct((2, 4, RING, rows, size), bf16),
        ]
        buffers += [
            vmem((slots, 2, RING, rows // 2, size), bf16),
            vmem((slots, 2, RING, rows // 2, size), bf16),
            vmem((4, RING, rows, size), bf16),
            vmem((2, RING, rows, size), bf16),
            vmem((2, RING, rows // 2, size), bf16),
            vmem((2, RING, rows, size), bf16),
            vmem((2, rows // 2, size), bf16),
            vmem((2, rows, size), bf16),
        ]
    return landing, buffers


def experts_kernel(
    cuts,
    x_all,
    dy_all,
    w_own,
    w_pair,
    resid,
    chances,
    router,
    ffn_norm,
    cot,
    d_resid,
    out_mine,
    d_resid_mine,
    small_rows,
    grad_experts,
    grad_down,
    xs,
    ds,
    act,
    ret,
    pair_in,
    *refs,
):
    f32, bf16 = jnp.float32, jnp.bfloat16
    hbm, refs = refs[:6], refs[6:]
    bufs, refs = refs[:24], refs[24:]
    (
        home,
        stage,
        cot_now,
        send_sems,
        recv_sems,
        ring_sems,
        load_sems,
        store_sems,
        weight_sems,
        cot_sem,
        grad_load_sems,
        grad_pair_sems,
        grad_store_sems,
    ) = refs
    links = Links((X, Z, Y), send_sems, recv_sems, pair=True)
    here_x, here_z, here_y = links.at
    rows = ret.shape[3]
    width = resid.shape[1]
    ff = act.shape[2] // 3
    cap = CAP
    locals_ = xs.shape[0]
    half_experts = locals_ // 2
    group = (here_x * RING + here_z) * 2
    ids = [(group + links.core) * half_experts + j for j in range(half_experts)]
    ids += [(group + 1 - links.core) * half_experts + j for j in range(half_experts)]

    cot_rows = cot.at[pl.ds(pl.multiple_of(here_y * rows, rows), rows)]
    cot_load = pltpu.make_async_copy(cot_rows, cot_now, cot_sem)
    cot_load.start()

    def group_at(s, g):
        gx = lax.rem(here_x + far_first(s) + RING, RING)
        gz = lax.rem(here_z + far_first(g) + RING, RING)
        return gx, gz

    rings = ring_sums(links, ret, cuts, ORDERS, hbm, bufs, ring_sems)

    def act_at(key, work=None):
        act_on(rings, PLAN[key], work)

    def bring_home():
        for p, (start, size) in enumerate(cuts):
            home[:, start : start + size] = bufs[8 * p + 2][3, links.at[ORDERS[p][2]]]

    lane = lax.broadcasted_iota(jnp.int32, (2 * locals_, 128), 1)
    row = lax.broadcasted_iota(jnp.int32, (2 * locals_, 128), 0)
    select = jnp.zeros((2 * locals_, 128), f32)
    for j in range(locals_):
        select = jnp.where((row == j) & (lane == ids[j] + EXPERTS), 1.0, select)
        select = jnp.where((row == locals_ + j) & (lane == ids[j]), 1.0, select)
    select = select.astype(bf16)
    before = jnp.where(
        lax.broadcasted_iota(jnp.int32, (TOK, TOK), 0)
        < lax.broadcasted_iota(jnp.int32, (TOK, TOK), 1),
        1.0,
        0.0,
    ).astype(bf16)
    slots = lax.broadcasted_iota(jnp.int32, (cap, TOK), 0).astype(f32)
    out_lane = lax.broadcasted_iota(jnp.int32, (RING * cap, 128), 1)
    def groups(weights, x, dy, xs_now, ds_now, act_now, places, terms, ret_now):
        def weight_loads():
            return [
                pltpu.make_async_copy(w_own, weights.at[0], weight_sems.at[0]),
                pltpu.make_async_copy(w_pair, weights.at[1], weight_sems.at[1]),
            ]

        for copy in weight_loads():
            copy.start()

        def loads(s, g):
            gx, gz = group_at(s, g)
            return [
                pltpu.make_async_copy(x_all.at[gx, gz], x.at[g % 2], load_sems.at[g % 2, 0]),
                pltpu.make_async_copy(dy_all.at[gx, gz], dy.at[g % 2], load_sems.at[g % 2, 1]),
            ]

        def rows_of(s):
            start = s * RING * cap
            if not isinstance(s, int):
                start = pl.multiple_of(start, RING * cap)
            return pl.ds(start, RING * cap)

        def row_stores(s):
            return [
                pltpu.make_async_copy(xs_now, xs.at[:, rows_of(s)], store_sems.at[0]),
                pltpu.make_async_copy(ds_now, ds.at[:, rows_of(s)], store_sems.at[1]),
            ]

        def act_store(s):
            return pltpu.make_async_copy(act_now, act.at[:, rows_of(s)], store_sems.at[2])

        def ret_store(s, g):
            gx, gz = group_at(s, g)
            dst = ret.at[gx, gz, :, :, pl.ds(0, width + 128)]
            return pltpu.make_async_copy(ret_now.at[g % 2], dst, store_sems.at[3 + g % 2])

        def ret_y_store(s, g):
            gx, gz = group_at(s, g)
            src = ret_now.at[g % 2, :, :, pl.ds(0, width)]
            dst = ret.at[gx, gz, :, :, pl.ds(width + 128, width)]
            return pltpu.make_async_copy(src, dst, store_sems.at[3 + g % 2])

        def sums_at(s, point):
            for k in range(RING):
                if (k, point) in PLAN:
                    pl.when(s == k)(functools.partial(act_at, (k, point)))

        for g in range(2):
            for copy in loads(0, g):
                copy.start()

        @pl.loop(0, RING)
        def _(s):
            gates = []

            @pl.when(s > 0)
            def _():
                for copy in row_stores(s):
                    copy.wait()

            for g in range(RING):
                for copy in loads(s, g):
                    copy.wait()
                marks = x[g % 2, :, :, width:].reshape(TOK, 128)
                flags = dot(select, marks, NT)
                slot = dot(flags.astype(bf16), before, NN)
                place, gate = [], []
                for j in range(locals_):
                    hit = (slots == slot[j : j + 1]) & (flags[j : j + 1] > 0.5)
                    place.append(jnp.where(hit, 1.0, 0.0))
                    chance = flags[locals_ + j : locals_ + j + 1]
                    gate.append(jnp.sum(place[-1] * chance, axis=1, keepdims=True))
                place = jnp.concatenate(place, axis=0).astype(bf16)
                places[g] = place
                gates.append(gate)
                picked = dot(place, x[g % 2, :, :, :width].reshape(TOK, width), NN).astype(bf16)
                for j in range(locals_):
                    xs_now[j, g * cap : (g + 1) * cap, :] = picked[j * cap : (j + 1) * cap]
                picked = dot(place, dy[g % 2].reshape(TOK, width), NN).astype(bf16)
                for j in range(locals_):
                    ds_now[j, g * cap : (g + 1) * cap, :] = picked[j * cap : (j + 1) * cap]
                if g < 2:
                    for copy in loads(s, g + 2):
                        copy.start()
                else:

                    @pl.when(s < RING - 1)
                    def _():
                        for copy in loads(s + 1, g - 2):
                            copy.start()

            for copy in row_stores(s):
                copy.start()

            @pl.when(s == 0)
            def _():
                for copy in weight_loads():
                    copy.wait()

            @pl.when(s > 0)
            def _():
                act_store(s).wait()
                for g in range(2):
                    ret_y_store(s, g).wait()

            sums_at(s, 0)
            for j in range(locals_):
                if j == half_experts:
                    sums_at(s, 1)
                w = weights.at[j // half_experts, j % half_experts]
                gate = jnp.concatenate([gates[g][j] for g in range(RING)], axis=0)
                up_in = dot(xs_now[j], w[0], NN)
                up = dot(xs_now[j], w[1], NN)
                d_raw = dot(ds_now[j], w[2], NN)
                sig = 1.0 / (1.0 + jnp.exp(-up_in))
                silu = up_in * sig
                hidden = (silu * up).astype(bf16).astype(f32)
                d_gate = jnp.sum(hidden * d_raw, axis=1, keepdims=True)
                d_hidden = d_raw * gate
                act_now[j, :, :ff] = (hidden * gate).astype(bf16)
                act_now[j, :, ff : 2 * ff] = (
                    d_hidden * up * sig * (1.0 + up_in * (1.0 - sig))
                ).astype(bf16)
                act_now[j, :, 2 * ff :] = (d_hidden * silu).astype(bf16)
                dg = jnp.where(out_lane == ids[j], d_gate, 0.0).astype(bf16)
                dx = dot(act_now[j, :, ff : 2 * ff], w[0], NT)
                dx = (dx + dot(act_now[j, :, 2 * ff :], w[1], NT)).astype(bf16)
                for g in range(RING):
                    part = slice(g * cap, (g + 1) * cap)
                    there = slice(j * cap, (j + 1) * cap)
                    terms[g, there, :width] = dx[part]
                    terms[g, there, width:] = dg[part]
            act_store(s).start()
            for g in range(RING):
                if g >= 2:
                    ret_store(s, g - 2).wait()
                ret_now[g % 2] = (
                    dot(places[g], terms[g], TN).astype(bf16).reshape(RING, rows, width + 128)
                )
                ret_store(s, g).start()
            for j in range(locals_):
                if j == half_experts:
                    for g in range(2):
                        ret_store(s, g).wait()
                    sums_at(s, 2)
                w = weights.at[j // half_experts, j % half_experts]
                y = dot(act_now[j, :, :ff], w[2], NT).astype(bf16)
                for g in range(RING):
                    terms[g, j * cap : (j + 1) * cap, :width] = y[g * cap : (g + 1) * cap]
            for g in range(RING):
                if g >= 2:
                    ret_y_store(s, g - 2).wait()
                ret_now[g % 2, :, :, :width] = (
                    dot(places[g], terms[g, :, :width], TN).astype(bf16).reshape(RING, rows, width)
                )
                ret_y_store(s, g).start()

        for g in range(2):
            ret_y_store(0, g).wait()
        for copy in row_stores(0) + [act_store(0)]:
            copy.wait()

    wide = x_all.shape[4]
    pl.run_scoped(
        groups,
        pltpu.VMEM((2,) + w_own.shape, bf16),
        pltpu.VMEM((2, RING, rows, wide), bf16),
        pltpu.VMEM((2, RING, rows, width), bf16),
        pltpu.VMEM((locals_, RING * cap, width), bf16),
        pltpu.VMEM((locals_, RING * cap, width), bf16),
        pltpu.VMEM((locals_, RING * cap, 3 * ff), bf16),
        pltpu.VMEM((RING, locals_ * cap, TOK), bf16),
        pltpu.VMEM((RING, locals_ * cap, width + 128), bf16),
        pltpu.VMEM((2, RING, rows, width + 128), bf16),
    )

    def ending(xs_e, ds_e, act_e, given, taken, summed):
        def loads(j):
            e = (j + half_experts) % locals_
            return [
                pltpu.make_async_copy(src.at[e], dst.at[j % 2], grad_load_sems.at[j % 2, i])
                for i, (src, dst) in enumerate(((xs, xs_e), (ds, ds_e), (act, act_e)))
            ]

        def take(n):
            return pltpu.make_async_copy(
                pair_in.at[n // 3, n % 3], taken.at[n % 2], grad_pair_sems.at[n % 2]
            )

        def store(n):
            e, i = n // 3, n % 3
            dst = grad_down.at[e] if i == 2 else grad_experts.at[e, i]
            return pltpu.make_async_copy(summed.at[n % 2], dst, grad_store_sems.at[n % 2])

        sent = []

        def work():
            for copy in loads(0):
                copy.start()
            for j in range(locals_):
                for copy in loads(j):
                    copy.wait()
                if j + 1 < locals_:
                    for copy in loads(j + 1):
                        copy.start()
                for i in range(3):
                    rows_in = ds_e if i == 2 else xs_e
                    cols_in = (slice(ff, 2 * ff), slice(2 * ff, 3 * ff), slice(0, ff))[i]
                    n = (j % half_experts) * 3 + i
                    own = j >= half_experts
                    if own:
                        links.arrive(sent[n], pair_in.at[n // 3, n % 3])
                        take(n).start()
                        if n >= 2:
                            store(n - 2).wait()
                        take(n).wait()

                    @pl.loop(0, RING)
                    def _(q):
                        cut = pl.ds(pl.multiple_of(q * (width // RING), width // RING), width // RING)
                        part = dot(rows_in[j % 2, :, cut], act_e[j % 2, :, cols_in], TN)
                        if own:
                            part = part + taken[n % 2, cut, :].astype(f32)
                            summed[n % 2, cut, :] = part.astype(bf16)
                        else:
                            given[n, cut, :] = part.astype(bf16)

                    if own:
                        store(n).start()
                    else:
                        sent.append(
                            links.send(given.at[n], pair_in.at[n // 3, n % 3], links.pair())
                        )
                    yield

        piece = work()
        act_at((RING, 0), piece)
        for _ in go_on():
            pass
        run_all([piece])
        for n in (3 * half_experts - 2, 3 * half_experts - 1):
            store(n).wait()
        for k in sent:
            links.sent(k, given.at[0])
        links.close()

    def go_on():
        bring_home()
        cot_load.wait()
        values = resid[...]
        inverse = lax.rsqrt(jnp.mean(values * values, axis=-1, keepdims=True) + EPSILON)
        hat = values * inverse
        moe_in = (hat * ffn_norm[...]).astype(bf16)
        probs, picks = chances[:, :EXPERTS], chances[:, EXPERTS:]
        d_probs = home[:, width : width + EXPERTS].astype(f32) * picks
        d_logits = probs * (d_probs - jnp.sum(probs * d_probs, axis=-1, keepdims=True))
        d_logits = d_logits.astype(bf16)
        d_moe = home[:, :width].astype(f32) + dot(d_logits, router[...], NN)
        d_hat = d_moe * ffn_norm[...]
        final = cot_now[...].astype(f32) + inverse * (
            d_hat - hat * jnp.mean(d_hat * hat, axis=-1, keepdims=True)
        )
        d_resid_mine[...] = final
        stage[...] = final.astype(bf16)
        here = pl.ds(pl.multiple_of(here_y * rows, rows), rows)
        copy = pltpu.make_async_copy(stage, d_resid.at[here], cot_sem)
        copy.start()

        def view(places, half):
            start = places[Y] * rows + (0 if half is None else half * (rows // 2))
            size = rows if half is None else rows // 2
            return d_resid.at[pl.ds(pl.multiple_of(start, size), size)]

        sharing = gather_part(links, view, stage, (Y,))
        next(sharing)
        out_mine[...] = (values + home[:, width + 128 :].astype(f32)).astype(bf16)
        small_rows[:EXPERTS, :] = dot(d_logits, moe_in, TN)
        row = lax.broadcasted_iota(jnp.int32, (8, width), 0)
        d_ffn = jnp.sum(d_moe * hat, axis=0, keepdims=True)
        small_rows[EXPERTS:, :] = jnp.where(row == 1, d_ffn, 0.0)
        yield
        next(sharing)
        next(sharing)
        yield
        run_all([sharing])
        copy.wait()

    chunk = xs.shape[1:]
    pl.run_scoped(
        ending,
        pltpu.VMEM((2,) + chunk, bf16),
        pltpu.VMEM((2,) + chunk, bf16),
        pltpu.VMEM((2,) + act.shape[1:], bf16),
        pltpu.VMEM((3 * half_experts, width, ff), bf16),
        pltpu.VMEM((2, width, ff), bf16),
        pltpu.VMEM((2, width, ff), bf16),
    )


def experts(x_all, dy_all, w_own, w_pair, resid, chances, router, ffn_norm, cot, collective_id):
    rows, wide = x_all.shape[3:]
    width = dy_all.shape[4]
    ff = w_own.shape[3]
    locals_ = 2 * w_own.shape[0]
    groups = RING * RING
    bf16, f32 = jnp.bfloat16, jnp.float32
    cols = 2 * width + 128
    cuts = cut_as(*TILES)
    vmem, dma = pltpu.VMEM, pltpu.SemaphoreType.DMA
    shape = jax.ShapeDtypeStruct
    hbm_out, bufs = ring_buffers(rows, cuts)
    in_vmem = pl.BlockSpec(memory_space=vmem)
    in_hbm = pl.BlockSpec(memory_space=pltpu.HBM)
    return pl.pallas_call(
        functools.partial(experts_kernel, cuts),
        in_specs=[in_hbm] * 4 + [in_vmem] * 4 + [in_hbm],
        out_specs=[in_hbm] + [in_vmem] * 3 + [in_hbm] * 13,
        out_shape=[
            shape((RING * rows, width), bf16),
            shape((rows, width), bf16),
            shape((rows, width), f32),
            shape((EXPERTS + 8, width), f32),
            shape((locals_ // 2, 2, width, ff), bf16),
            shape((locals_ // 2, width, ff), bf16),
            shape((locals_, groups * CAP, width), bf16),
            shape((locals_, groups * CAP, width), bf16),
            shape((locals_, groups * CAP, 3 * ff), bf16),
            shape((RING, RING, RING, rows, cols), bf16),
            shape((locals_ // 2, 3, width, ff), bf16),
        ]
        + hbm_out,
        scratch_shapes=bufs
        + [
            vmem((rows, cols), bf16),
            vmem((rows, width), bf16),
            vmem((rows, width), bf16),
            dma((118,)),
            dma((118,)),
            dma((3, 4, 7)),
            dma((2, 2)),
            dma((5,)),
            dma((2,)),
            dma,
            dma((2, 3)),
            dma((2,)),
            dma((2,)),
        ],
        compiler_params=pltpu.CompilerParams(
            collective_id=collective_id, has_side_effects=True, vmem_limit_bytes=VMEM_LIMIT
        ),
        cost_estimate=pl.CostEstimate(flops=0, bytes_accessed=0, transcendentals=0),
        name="experts",
    )(x_all, dy_all, w_own, w_pair, resid, chances, router, ffn_norm, cot)


def reduce_plane_part(links, order, region, pair_in, bufs):
    pass_a, land_a, pass_b, land_b = bufs
    a1, a2 = order
    steps = (2, 1, -1, 0)
    given = []
    for i, step in enumerate(steps):
        places = {a1: links.rel(a1, step)}
        src = region(places, 1 - links.core)
        given.append(links.send(src, pair_in.at[i], links.pair()))
    yield
    mine = {}
    for i, step in enumerate(steps):
        mine[step] = region({a1: links.rel(a1, step)}, links.core)
        links.arrive(given[i], pair_in.at[i])
        add_into(mine[step], pair_in.at[i])
    yield from reduce_small(links, a1, lambda step: mine[step], mine[0], pass_a, land_a)
    yield

    def at(step):
        return region({a1: links.at[a1], a2: links.rel(a2, step)}, links.core)

    yield from reduce_small(links, a2, at, at(0), pass_b, land_b)


def plane_buffers(rows, size):
    return [
        pltpu.VMEM(shape, jnp.bfloat16)
        for shape in (
            (4, RING, rows, size),
            (2, RING, rows // 2, size),
            (2, RING, rows, size),
            (2, rows // 2, size),
            (2, rows, size),
        )
    ]


def back_kernel(
    lengths,
    d_resid,
    all_weights,
    heads,
    raw,
    stats,
    lse,
    mixed,
    normed,
    tokens,
    attn_norm,
    q_gain,
    k_gain,
    d_resid_mine,
    small_rows,
    out_mine,
    freqs,
    input_grad,
    out,
    grad_qkv,
    grad_out,
    grad_router,
    grad_attn,
    grad_ffn,
    grad_q,
    grad_k,
    terms,
    d_mixed,
    d_rot,
    d_proj,
    sums,
    sums_in,
    parts,
    passing,
    landing,
    d_normed,
    grads_in,
    rows_small,
    held,
    small_in,
    whole,
    row_sum,
    row_out,
    row_in,
    row_in_x,
    row_in_z,
    row_in_pair,
    *rest,
):
    f32, bf16 = jnp.float32, jnp.bfloat16
    bufs, (weights, send_sems, recv_sems, local_sem, weight_sems) = rest[:-5], rest[-5:]
    cols = q_gain.shape[1]

    def weight_load(j):
        cut = pl.ds(0, 3 * cols) if j else pl.ds(3 * cols, cols)
        at = (slice(None),) * 4 + (cut,)
        return pltpu.make_async_copy(all_weights.at[at], weights.at[at], weight_sems.at[j])

    for j in range(2):
        weight_load(j).start()
    links = Links((X, Z, Y), send_sems, recv_sems, pair=True, extra=[(Y, 2), (X, 2), (Z, 2)])
    x, z, y = links.at
    core = links.core
    rows, width = tokens.shape
    quarter = rows // RING
    block_rows = terms.shape[3]
    mine = pl.ds(pl.multiple_of(y * quarter, quarter), quarter)
    out_here = pltpu.make_async_copy(out_mine, out.at[mine], local_sem)
    out_here.start()

    def out_view(places, half):
        size = quarter if half is None else quarter // 2
        start = places[Y] * quarter + (half or 0) * size
        return out.at[pl.ds(pl.multiple_of(start, size), size)]

    out_sharing = gather_part(links, out_view, out_mine, (Y,))
    position, allowed = packed_layout(lengths)
    cosine, sine = rope_rows(position, freqs[...])
    scale = HEAD ** (-0.5)

    def weight(start, stop):
        return weights[:, :, :, :, start:stop].reshape(width, stop - start)

    weight_load(0).wait()
    d_mixed[...] = dot(d_resid[...], weight(3 * cols, 4 * cols), NN).astype(bf16)
    rows_small[...] = jnp.zeros(rows_small.shape, f32)
    rows_small[: small_rows.shape[0], :] = small_rows[...]
    means = [jnp.zeros((rows, 1), f32), jnp.zeros((rows, 1), f32)]
    for h in range(cols // HEAD):
        own = slice(h * HEAD, (h + 1) * HEAD)
        query, key, value = (
            heads[:, j * cols + h * HEAD : j * cols + (h + 1) * HEAD] for j in range(3)
        )
        scores = dot(query, key, NT) * scale
        probs = jnp.exp(jnp.where(allowed, scores, -1e30) - lse[:, h : h + 1])
        probs = jnp.where(allowed, probs, 0.0)
        d_out = d_mixed[:, own]
        d_proj[:, 2 * cols + h * HEAD : 2 * cols + (h + 1) * HEAD] = dot(
            probs.astype(bf16), d_out, TN
        ).astype(bf16)
        d_probs = dot(d_out, value, NT)
        d_scores = probs * (d_probs - jnp.sum(probs * d_probs, axis=-1, keepdims=True))
        d_scores = d_scores.astype(bf16)
        turned = (dot(d_scores, key, NN) * scale, dot(d_scores, query, TN) * scale)
        for j, (grad, gain) in enumerate(zip(turned, (q_gain, k_gain))):
            at = slice(j * cols + h * HEAD, j * cols + (h + 1) * HEAD)
            grad = grad * cosine - swap(grad) * sine
            hat = raw[:, at] * stats[:, j : j + 1]
            place_at = pl.ds(pl.multiple_of(y * cols + h * HEAD, HEAD), HEAD)
            rows_small[66 + j : 67 + j, place_at] = jnp.sum(grad * hat, axis=0, keepdims=True)
            grad = grad * gain[:, own]
            d_rot[:, at] = grad
            means[j] = means[j] + jnp.sum(grad * hat, axis=-1, keepdims=True)
    sent = start_sums(links, means, sums, sums_in)

    def fill(left, right, start):
        size = right.shape[1]

        @pl.loop(0, RING)
        def _(i):
            block = 2 * RING * block_rows
            some = left[:, pl.ds(pl.multiple_of(i * block, block), block)]
            terms[i, :, :, :, start : start + size] = (
                dot(some, right, TN).astype(bf16).reshape(RING, 2, block_rows, size)
            )

    def region(cut, places, at_core):
        index = tuple(places.get(axis, slice(None)) for axis in (X, Z))
        return terms.at[index + (at_core, slice(None), cut)]

    def reduction(part, start, size, order):
        own = bufs[5 * part : 5 * part + 5]
        cut = pl.ds(start, size)
        return reduce_plane_part(links, order, functools.partial(region, cut), own[0], own[1:])

    wide = 4 * cols
    small_cols = rows_small.shape[0]
    terms[:, :, :, :, wide:] = (
        rows_small[...].T.astype(bf16).reshape(RING, RING, 2, block_rows, small_cols)
    )
    fill(normed, d_proj[:, 2 * cols :], 2 * cols)
    fill(d_resid, mixed[...], 3 * cols)
    first = reduction(0, 2 * cols, 2 * cols + small_cols, (X, Z))
    next(first)
    total = end_sums(links, sent, sums, sums_in) / (HEADS * HEAD)
    for j in range(2):
        at = slice(j * cols, (j + 1) * cols)
        inverse = stats[:, j : j + 1]
        hat = raw[:, at] * inverse
        d_proj[:, at] = (inverse * (d_rot[:, at] - hat * total[:, j : j + 1])).astype(bf16)
    fill(normed, d_proj[:, : 2 * cols], 0)
    second = reduction(1, 0, 2 * cols, (Z, X))
    next(second)
    next(first)

    def quarter_rows(step):
        return pl.ds(pl.multiple_of(links.rel(Y, step) * quarter, quarter), quarter)

    weight_load(1).wait()
    whole[...] = dot(d_proj[...], weight(0, 3 * cols), NT)
    for k, step in enumerate((2, 1, -1)):
        parts[k] = whole[quarter_rows(step), :].astype(bf16)
    d_normed[...] = whole[mine, :]
    by_step = {2: parts.at[0], 1: parts.at[1], -1: parts.at[2]}
    summing = reduce_small(links, Y, by_step.get, d_normed, passing, landing)
    next(summing)
    next(second)
    next(first)
    next(summing)
    next(second)
    next(first)
    run_all([summing])
    hidden = tokens[mine, :].astype(f32)
    inverse = lax.rsqrt(jnp.mean(hidden * hidden, axis=-1, keepdims=True) + EPSILON)
    hat = hidden * inverse
    row_sum[...] = jnp.sum(d_normed[...] * hat, axis=0, keepdims=True)
    row_out[3] = row_sum[...]
    sent_row = [
        links.send(row_out.at[3], row_in.at[k], links.peer(Y, k + 1)) for k in range(3)
    ]
    d_hat = d_normed[...] * attn_norm[...]
    final = d_resid_mine[...] + inverse * (
        d_hat - hat * jnp.mean(d_hat * hat, axis=-1, keepdims=True)
    )
    grads_in[y] = final.astype(bf16)

    def grads_view(places, half):
        if half is None:
            return grads_in.at[places[Y]]
        return grads_in.at[places[Y], pl.ds(half * (quarter // 2), quarter // 2)]

    sharing = gather_part(links, grads_view, grads_in.at[y], (Y,))
    next(sharing)
    next(out_sharing)

    def row_add(sent, landed):
        for k in range(3):
            links.arrive(sent[k], landed.at[k])
        row_sum[...] = row_sum[...] + landed[0] + landed[1] + landed[2]

    def row_on(axis, landed):
        row_out[axis] = row_sum[...]
        return [
            links.send(row_out.at[axis], landed.at[k], links.peer(axis, step))
            for k, step in enumerate((2, 1, -1))
        ]

    run_all([first])
    here = terms.at[x, z, core]
    small = here.at[:, pl.ds(wide, small_cols)]
    sent = [links.send(small, small_in.at[k], links.peer(Y, k + 1)) for k in range(3)]
    row_add(sent_row, row_in)
    sent_row = row_on(X, row_in_x)
    next(second)
    next(sharing)
    total = small[...].astype(f32)
    for k in range(3):
        links.arrive(sent[k], small_in.at[k])
        total = total + small_in[k].astype(f32)
    held[x, z, core] = total.astype(bf16)
    own = held.at[x, z, core]
    sent = [links.send(own, own, links.peer(X, step)) for step in (2, 1, -1)]
    grad_out[...] = here[:, 3 * cols : 4 * cols].astype(f32)
    grad_qkv[2] = here[:, 2 * cols : 3 * cols].astype(f32)
    row_add(sent_row, row_in_x)
    sent_row = row_on(Z, row_in_z)
    for k, step in zip(sent, (2, 1, -1)):
        links.arrive(k, held.at[links.rel(X, -step), z, core])
    own = held.at[:, z, core]
    sent = [links.send(own, own, links.peer(Z, step)) for step in (2, 1, -1)]
    next(second, None)
    next(sharing)
    next(out_sharing)
    row_add(sent_row, row_in_z)
    row_out[Y] = row_sum[...]
    sent_row = links.send(row_out.at[Y], row_in_pair, links.pair())
    for k, step in zip(sent, (2, 1, -1)):
        links.arrive(k, held.at[:, links.rel(Z, -step), core])
    own = held.at[:, :, core]
    k = links.send(own, own, links.pair())
    run_all([second, sharing, out_sharing])
    for j in range(2):
        grad_qkv[j] = here[:, j * cols : (j + 1) * cols].astype(f32)
    for q in range(RING):
        input_grad[q * quarter : (q + 1) * quarter, :] = grads_in[q]
    links.arrive(k, held.at[:, :, 1 - core])
    rows_small[...] = held[...].astype(f32).reshape(width, small_cols).T
    grad_router[...] = rows_small[:EXPERTS, :]
    links.arrive(sent_row, row_in_pair)
    grad_attn[...] = row_sum[...] + row_in_pair[...]
    grad_ffn[...] = rows_small[65:66, :]
    out_here.wait()
    cut = pl.ds(pl.multiple_of(y * cols, cols), cols)
    grad_q[...] = rows_small[66:67, cut]
    grad_k[...] = rows_small[67:68, cut]
    links.close()


def back(
    lengths,
    d_resid,
    weights,
    heads,
    raw,
    stats,
    lse,
    mixed,
    normed,
    tokens,
    attn_norm,
    q_gain,
    k_gain,
    d_resid_mine,
    small_rows,
    out_mine,
    collective_id,
):
    bf16, f32 = jnp.bfloat16, jnp.float32
    rows, width = tokens.shape
    cols = q_gain.shape[1]
    quarter = rows // RING
    block_rows = weights.shape[3]
    half = HEAD // 2
    freqs = 10000.0 ** (-jnp.arange(half, dtype=f32) / half)
    freqs = jnp.concatenate([freqs, freqs])[None, :]
    in_vmem = pl.BlockSpec(memory_space=pltpu.VMEM)
    shape = jax.ShapeDtypeStruct
    in_hbm = pl.BlockSpec(memory_space=pltpu.HBM)
    vmem = pltpu.VMEM
    buffers = []
    for size in (2 * cols + 128, 2 * cols):
        buffers += plane_buffers(block_rows, size)
    return pl.pallas_call(
        back_kernel,
        in_specs=[pl.BlockSpec(memory_space=pltpu.SMEM), in_vmem, in_hbm] + [in_vmem] * 14,
        out_specs=[in_vmem, in_hbm] + [in_vmem] * 7,
        out_shape=[
            shape((rows, width), bf16),
            shape((rows, width), bf16),
            shape((3, block_rows, cols), f32),
            shape((block_rows, cols), f32),
            shape((EXPERTS, width), f32),
            shape((1, width), f32),
            shape((1, width), f32),
            shape((1, cols), f32),
            shape((1, cols), f32),
        ],
        scratch_shapes=[
            vmem((RING, RING, 2, block_rows, 4 * cols + 128), bf16),
            vmem((rows, cols), bf16),
            vmem((rows, 2 * cols), f32),
            vmem((rows, 3 * cols), bf16),
            vmem((8, rows), f32),
            vmem((3, 8, rows), f32),
            vmem((3, quarter, width), bf16),
            vmem((2, quarter // 2, width), bf16),
            vmem((2, quarter, width), bf16),
            vmem((quarter, width), f32),
            vmem((RING, quarter, width), bf16),
            vmem((128, width), f32),
            vmem((RING, RING, 2, block_rows, 128), bf16),
            vmem((3, block_rows, 128), bf16),
            vmem((rows, width), f32),
            vmem((1, width), f32),
            vmem((4, 1, width), f32),
            vmem((3, 1, width), f32),
            vmem((3, 1, width), f32),
            vmem((3, 1, width), f32),
            vmem((1, width), f32),
        ]
        + buffers
        + [
            vmem(weights.shape, bf16),
            pltpu.SemaphoreType.DMA((80,)),
            pltpu.SemaphoreType.DMA((80,)),
            pltpu.SemaphoreType.DMA,
            pltpu.SemaphoreType.DMA((2,)),
        ],
        compiler_params=pltpu.CompilerParams(
            collective_id=collective_id, has_side_effects=True, vmem_limit_bytes=VMEM_LIMIT
        ),
        cost_estimate=pl.CostEstimate(flops=0, bytes_accessed=0, transcendentals=0),
        name="back",
    )(
        lengths,
        d_resid,
        weights,
        heads,
        raw,
        stats,
        lse,
        mixed,
        normed,
        tokens,
        attn_norm,
        q_gain,
        k_gain,
        d_resid_mine,
        small_rows,
        out_mine,
        freqs,
    )


def body(
    tokens,
    attn_norm,
    qkv_weights,
    out_weight,
    q_gain,
    k_gain,
    ffn_norm,
    router,
    expert_weights,
    lengths,
    expert_ids,
    cotangent,
):
    pairs = [(i, i ^ 1) for i in range(lax.axis_size("expert"))]
    pair_weights = lax.ppermute(expert_weights, "expert", pairs)
    all_weights, rows_all, cot_rows, normed_b, heads, raw, inverses, lse, mixed_b, resid, chances = front(
        lengths,
        qkv_weights,
        out_weight,
        tokens,
        attn_norm[None],
        q_gain[None],
        k_gain[None],
        ffn_norm[None],
        router.T,
        expert_ids.T,
        cotangent,
        1,
    )
    d_resid, out_mine, d_resid_mine, small_rows, grad_experts, grad_down = experts(
        rows_all,
        cot_rows,
        expert_weights,
        pair_weights,
        resid,
        chances,
        router.T,
        ffn_norm[None],
        cotangent,
        3,
    )[:6]
    input_grad, output, grad_qkv, grad_out, grad_router, grad_attn, grad_ffn, grad_q, grad_k = back(
        lengths,
        d_resid,
        all_weights,
        heads,
        raw,
        inverses,
        lse,
        mixed_b,
        normed_b,
        tokens,
        attn_norm[None],
        q_gain[None],
        k_gain[None],
        d_resid_mine,
        small_rows,
        out_mine,
        4,
    )
    return (
        output,
        input_grad.astype(jnp.float32),
        grad_attn[0],
        grad_qkv,
        grad_out,
        grad_q[0],
        grad_k[0],
        grad_ffn[0],
        grad_router.T,
        grad_experts.astype(jnp.float32),
        grad_down.astype(jnp.float32),
    )


def solution(mesh):
    placed = (
        P(("dp", "expert"), None),
        P(),
        P(None, ("dp", "expert"), "mp"),
        P(("dp", "expert"), "mp"),
        P("mp"),
        P("mp"),
        P(),
        P(),
        P(("dp", "expert"), None, None, "mp"),
        P(("dp", "expert"), None),
        P(("dp", "expert"), None),
        P(("dp", "expert"), None),
    )
    return jax.shard_map(
        body,
        mesh=mesh,
        in_specs=placed,
        out_specs=(
            P(("dp", "expert"), None),
            P(("dp", "expert"), None),
            P(),
            P(None, ("dp", "expert"), "mp"),
            P(("dp", "expert"), "mp"),
            P("mp"),
            P("mp"),
            P(),
            P(),
            P(("dp", "expert"), None, None, "mp"),
            P(("dp", "expert"), None, "mp"),
        ),
        check_vma=False,
    )
```
